128 devices in a mesh: table: 32 (over x, y, core), blk: 4 (over z).
Axes of the slice: x: 4, y: 4, z: 4, core: 2. Of those that a mesh axis runs over, the one named last changes fastest.
Arguments:
- entity_table: bfloat16 [524288, 400], P(('table', 'blk')), may hold values from -6 to 6
- rel_center: bfloat16 [7424, 400], replicated, may hold values from -3 to 3
- rel_offset: bfloat16 [7424, 400], replicated, may hold values from -6 to 6
- entity_owner: int32 [32768, 2, 1], P(('table', 'blk')), may hold values from 0 to 127; in each aligned block of 512 rows (0 to 511, 512 to 1023, ..., all dimensions but the last counted through in order) at most 8 rows name the same one
- entity_row: int32 [32768, 2], P(('table', 'blk')), may hold values from 0 to 4095
- rel_ids: int32 [32768, 3], P(('table', 'blk')), may hold values from 0 to 7423
- query_type: int32 [32768], P(('table', 'blk')), may hold values from 0 to 2
- neg_rows: int32 [4096], P(('table', 'blk')), may hold values from 0 to 4095
Outputs:
- entity_grad: float32 [524288, 400], P(('table', 'blk'))
The draws below stay inside these ranges and needn't reach their ends.
Inputs may be any that keep to these rules, and one draw needn't show every extreme that they name: `entity_owner`: among the 512 anchor and answer entries of one device no owner is named more than 8 times; in some devices' entries an owner is named exactly 8 times.
All inputs are finite; a program needn't handle non-finite values.
Results may differ from the reference program's by a relative error of at most 0.0003.
Values may be sent and summed in bfloat16 or wider, within the bound.
A program may use at most 128 MiB of HBM per device.

```python
import math
import jax
import jax.numpy as jnp
import numpy as np
from jax import lax

D = 400
REL = 7424
HOPS = 3
ENT_DEV = 4096
Q_DEV = 256
POOL = 32
SLOT = 8
QUERIES = 32768
ENTITIES = 524288
NEGS = 4096
N_TABLE = 32
N_BLK = 4
DEVICES = 128


def plant(values, own_key, smallest, largest):
    extent = values.shape
    place = [jax.random.randint(jax.random.fold_in(own_key, axis), (), 0, extent[axis]) for axis in range(len(extent))]
    values = values.at[tuple(place)].set(smallest)
    longest = extent.index(max(extent))
    place[longest] = (place[longest] + 1) % extent[longest]
    return values.at[tuple(place)].set(largest)


def levels(stream_key, extent, split, least, high):
    gain = 1.0
    for axis_at, shards_of in split:
        draws = jax.random.uniform(jax.random.fold_in(jax.random.fold_in(stream_key, 6), axis_at), (shards_of,), jnp.float32, least / len(split), high / len(split))
        gain = gain * jnp.repeat(jnp.exp(draws), extent[axis_at] // shards_of).reshape((-1,) + (1,) * (len(extent) - 1 - axis_at))
    return gain


def shared_out(key, own, number, rows, count, top, most, lean):
    ranking = jax.random.permutation(key, count)
    packed, common = portions_of(count, rows * top, most, lean, True), portions_of(count, rows * top, most, lean, False)
    places = jnp.arange(count)

    def named(sizes, rotation):
        used = int((sizes > 0).sum())
        fixed = max(1, used // 4)
        passed = fixed + (places - fixed + rotation * (used - fixed)) % max(1, count - fixed)
        return jnp.zeros((count,), jnp.int32).at[ranking[jnp.where(places < fixed, places, passed)]].set(jnp.asarray(sizes, jnp.int32))

    sizes = jnp.where(number % 4 == 0, named(packed, number // 4), named(common, number - number // 4 - 1))
    mixed = jax.random.permutation(jax.random.fold_in(own, 3), count)
    donor, taker = mixed[0:count // 2 * 2:2], mixed[1:count // 2 * 2:2]
    margin = jnp.minimum(sizes[donor] - 1, most - sizes[taker]) // 2
    margin = jnp.where((donor == ranking[0]) | (taker == ranking[0]) | (sizes[taker] == 0), 0, jnp.maximum(margin, 0))
    passed = jax.random.randint(jax.random.fold_in(own, 4), (count // 2,), 0, 1 << 20) % (margin + 1)
    sizes = sizes.at[donor].add(-passed).at[taker].add(passed)
    labels = jnp.searchsorted(jnp.cumsum(sizes), jnp.arange(rows * top), side="right").astype(jnp.int32)
    listing = labels.reshape(top, rows).T
    listing = listing[jax.random.permutation(jax.random.fold_in(own, 1), rows)]
    rotation = jax.random.randint(jax.random.fold_in(own, 2), (rows, 1), 0, top)
    return jnp.take_along_axis(listing, (jnp.arange(top)[None, :] + rotation) % top, axis=1)


def portions_of(number_of, total, most, skew, full):
    weights = [(1 << 20) // math.isqrt(standing ** skew) + 1 for standing in range(1, number_of + 1)]
    largest = most if full else min(most, max(-(-total // number_of), total * weights[0] // sum(weights)))
    least = 1 if total - largest >= number_of - 1 else 0
    holding, spare = [largest] + [least] * (number_of - 1), total - largest - least * (number_of - 1)
    while spare > 0:
        candidates = [i for i in range(1, number_of) if holding[i] < largest] or [i for i in range(1, number_of) if holding[i] < most]
        mass, left = sum([weights[i] for i in candidates]), spare
        for i in candidates:
            extra = min(most - holding[i], max(1, left * weights[i] // mass), spare)
            holding[i] = holding[i] + extra
            spare = spare - extra
    return np.array(holding)


def bell_draw(own_key, dims, scale, bound, shards=(), kind=jnp.bfloat16):
    entries = jax.random.normal(own_key, dims, jnp.float32) * scale
    if len(shards) > 0:
        entries = levels(own_key, dims, shards, -0.22, 0.18) * entries
    return jnp.clip(entries, min=-bound, max=bound).astype(kind)


def setup_inputs(seed: int = 0) -> dict:
    key_list = jax.random.split(jax.random.key(seed), 9)
    entity_table = bell_draw(key_list[0], (ENTITIES, D), 1.0, 6.0, ((0, 128),))
    rel_center = bell_draw(key_list[1], (REL, D), 0.5, 3.0)
    rel_offset = bell_draw(key_list[2], (REL, D), 1.0, 6.0)
    entity_owner_keys = jax.random.split(jax.random.fold_in(key_list[3], 1), QUERIES * 2 // (2 * Q_DEV))
    entity_owner_turns = jax.random.permutation(jax.random.fold_in(key_list[3], 3), QUERIES * 2 // (2 * Q_DEV))
    entity_owner = jax.vmap(lambda own, number: shared_out(jax.random.fold_in(key_list[3], 2), own, number, 2 * Q_DEV, DEVICES, 1, SLOT, 2))(entity_owner_keys, entity_owner_turns).reshape((QUERIES, 2, 1))
    entity_row = plant(jax.random.randint(key_list[4], (QUERIES, 2), 0, ENT_DEV), jax.random.fold_in(key_list[4], 1), 0, ENT_DEV - 1).astype(jnp.int32)
    rel_ids = plant(jax.random.randint(key_list[5], (QUERIES, HOPS), 0, REL), jax.random.fold_in(key_list[5], 1), 0, REL - 1).astype(jnp.int32)
    query_type = plant(jax.random.randint(key_list[6], (QUERIES,), 0, HOPS), jax.random.fold_in(key_list[6], 1), 0, HOPS - 1).astype(jnp.int32)
    neg_rows = plant(jax.random.randint(key_list[7], (NEGS,), 0, ENT_DEV), jax.random.fold_in(key_list[7], 1), 0, ENT_DEV - 1).astype(jnp.int32)
    return {"entity_table": entity_table, "rel_center": rel_center, "rel_offset": rel_offset, "entity_owner": entity_owner, "entity_row": entity_row, "rel_ids": rel_ids, "query_type": query_type, "neg_rows": neg_rows}


margin_gamma = 7.0
dist_scale = 0.02
inside_weight = 0.2
smooth_eps = 0.01
loss_scale = 64.0
query_block = 64

def box_distance(center, offset, entity):
    gap = entity - center
    spread = jnp.sqrt(gap * gap + smooth_eps)
    outside = jax.nn.softplus(spread - offset)
    inside = spread - outside
    return dist_scale * lax.optimization_barrier(jnp.sum(outside + inside_weight * inside, axis=-1))

def negative_loss(center, offset, entity):
    dist = box_distance(center[:, None, :], offset[:, None, :], entity[None, :, :])
    return -jnp.sum(jax.nn.log_sigmoid(dist - margin_gamma))

def positive_loss(center, offset, entity):
    dist = box_distance(center, offset, entity)
    return -jnp.sum(jax.nn.log_sigmoid(margin_gamma - dist))

def negative_grads(center, offset, entity, weight):
    blocks = center.shape[0] // query_block
    width = center.shape[1]

    def one_block(carry, pieces):
        value, pull = jax.vjp(negative_loss, pieces[0], pieces[1], entity)
        grad_center, grad_offset, grad_entity = pull(jnp.asarray(weight, value.dtype))
        return (carry + grad_entity, grad_center)
    start = jnp.zeros(entity.shape, entity.dtype)
    total, grad_center = lax.scan(one_block, start, (center.reshape(blocks, query_block, width), offset.reshape(blocks, query_block, width)))
    return (grad_center.reshape(center.shape), total)

def build_boxes(anchor, rel_center, rel_offset, rel_ids, query_type):
    centers = rel_center[rel_ids].astype(jnp.float32)
    offsets = jax.nn.softplus(rel_offset[rel_ids].astype(jnp.float32))
    hop_index = lax.broadcasted_iota(jnp.int32, rel_ids.shape, 1)
    active = (hop_index <= query_type[:, None]).astype(jnp.float32)[..., None]
    center = anchor.astype(jnp.float32) + lax.optimization_barrier(jnp.sum(active * centers, axis=1))
    offset = lax.optimization_barrier(jnp.sum(active * offsets, axis=1))
    return (center, offset)

def reference(entity_table, rel_center, rel_offset, entity_owner, entity_row, rel_ids, query_type, neg_rows):
    width = entity_table.shape[1]
    global_ids = (entity_owner[:, :, 0] * ENT_DEV + entity_row).astype(jnp.int32)
    picked = entity_table[global_ids]
    center, offset = build_boxes(picked[:, 0], rel_center, rel_offset, rel_ids, query_type)
    answer = picked[:, 1].astype(jnp.float32)
    value, pull = jax.vjp(positive_loss, center, offset, answer)
    pos_center, pos_offset, pos_entity = pull(jnp.asarray(loss_scale, value.dtype))
    group_queries = N_BLK * Q_DEV
    pool_size = N_BLK * POOL
    neg_ids = (lax.iota(jnp.int32, NEGS) // POOL * ENT_DEV + neg_rows).astype(jnp.int32)
    neg_entity = entity_table[neg_ids].astype(jnp.float32).reshape(N_TABLE, pool_size, width)
    weight = loss_scale / pool_size

    def one_group(pieces):
        return negative_grads(pieces[0], pieces[1], pieces[2], weight)
    neg_center, neg_grad = lax.map(one_group, (center.reshape(N_TABLE, group_queries, width), offset.reshape(N_TABLE, group_queries, width), neg_entity))
    gradient = jnp.zeros((ENTITIES, width), pos_center.dtype)
    gradient = gradient.at[global_ids[:, 0]].add(pos_center + neg_center.reshape(QUERIES, width))
    gradient = gradient.at[global_ids[:, 1]].add(pos_entity)
    gradient = gradient.at[neg_ids].add(neg_grad.reshape(NEGS, width))
    return gradient
```

```python
import functools
import math
import jax
import jax.numpy as jnp
from jax import lax
from jax.experimental import pallas as pl
from jax.experimental.pallas import tpu as pltpu
from jax.sharding import PartitionSpec as P

margin_gamma = 7.0
dist_scale = 0.02
inside_weight = 0.2
smooth_eps = 0.01
loss_scale = 64.0

f32 = jnp.float32
bf16 = jnp.bfloat16
i32 = jnp.int32
log2e = math.log2(math.e)
scaled_eps = smooth_eps * log2e * log2e
dist_unit = dist_scale * math.log(2.0) * inside_weight
log_weight = (1.0 - inside_weight) / inside_weight
slope_weight = 1.0 - inside_weight
lanes = 128
near = 8


def iota(shape, axis):
    return lax.broadcasted_iota(i32, shape, axis)


def dot(a, b, ca, cb):
    return lax.dot_general(a, b, (((ca,), (cb,)), ((), ())), preferred_element_type=f32)


def whole():
    return pl.BlockSpec(memory_space=pltpu.VMEM)


def params(mib, **more):
    return pltpu.CompilerParams(vmem_limit_bytes=mib * 2**20, **more)


def shifted(value, axis, steps):
    count = lax.axis_size(axis)
    pairs = [(source, (source + steps) % count) for source in range(count)]
    return lax.ppermute(value, axis, pairs)


def one_hot(mask):
    return jnp.where(mask, 1.0, 0.0).astype(bf16)


def slots_kernel(slot_count, devices, owner_ref, row_ref, wanted_ref, slot_ref):
    owner = jnp.concatenate([owner_ref[0:1, :], owner_ref[1:2, :]], axis=1)
    row = jnp.concatenate([row_ref[0:1, :], row_ref[1:2, :]], axis=1)
    requests = owner.shape[1]
    named = iota((devices, requests), 0) == owner
    named_hot = one_hot(named)
    earlier = one_hot(iota((requests, requests), 0) < iota((requests, requests), 1))
    before = dot(named_hot, earlier, 1, 0)
    rank = jnp.sum(jnp.where(named, before, 0.0), axis=0, keepdims=True).astype(i32)
    slot_ref[...] = owner * slot_count + rank
    high = lax.shift_right_logical(row, 6)
    low = row - high * 64
    ranked = iota((lanes, requests), 0) == rank
    high_hot = jnp.where(ranked, high.astype(f32), 0.0).astype(bf16)
    low_hot = jnp.where(ranked, low.astype(f32), 0.0).astype(bf16)
    asked = dot(named_hot, high_hot, 1, 1) * 64.0 + dot(named_hot, low_hot, 1, 1)
    wanted_ref[...] = asked.astype(i32)


def plan_slots(owner, row, slot_count, devices):
    requests = owner.shape[0] * owner.shape[1]
    return pl.pallas_call(
        functools.partial(slots_kernel, slot_count, devices),
        out_shape=(
            jax.ShapeDtypeStruct((devices, lanes), i32),
            jax.ShapeDtypeStruct((1, requests), i32),
        ),
        in_specs=[whole(), whole()],
        out_specs=(whole(), whole()),
        compiler_params=params(32),
        name="plan_slots",
    )(owner, row)


def asked_column(asked, slot_count):
    devices = asked.shape[0]
    rows = devices * slot_count
    high = lax.shift_right_logical(asked, 6)
    low = asked - high * 64
    group = lax.shift_right_logical(iota((rows, devices), 0), int(math.log2(slot_count)))
    pick = one_hot(group == iota((rows, devices), 1))
    spread = dot(pick, high.astype(f32).astype(bf16), 1, 0) * 64.0 + dot(
        pick, low.astype(f32).astype(bf16), 1, 0
    )
    mine = (iota((rows, lanes), 0) & (slot_count - 1)) == iota((rows, lanes), 1)
    return jnp.sum(jnp.where(mine, spread, 0.0), axis=1, keepdims=True).astype(i32)


def serve_kernel(slot_count, asked_ref, neg_ref, table_ref, served_ref, pool_ref, total, column):
    step = pl.program_id(0)
    part = table_ref.shape[1]
    rows = served_ref.shape[0]
    pool = pool_ref.shape[0]

    @pl.when(step == 0)
    def _():
        column[0:rows, :] = asked_column(asked_ref[...], slot_count)
        here = iota((pool, pool), 0) == iota((pool, pool), 1)
        column[rows : rows + pool, :] = jnp.sum(
            jnp.where(here, neg_ref[...].astype(f32), 0.0), axis=1, keepdims=True
        ).astype(i32)
        total[...] = jnp.zeros_like(total)

    base = step * part
    for start in range(0, rows + pool, 256):
        size = min(256, rows + pool - start)
        block = pl.ds(start, size)
        hot = one_hot(iota((size, part), 1) + base == column[block, :])
        total[block, :] += dot(hot, table_ref[...], 1, 1)

    @pl.when(step == pl.num_programs(0) - 1)
    def _():
        served_ref[...] = total[0:rows, :].astype(bf16)
        pool_ref[...] = total[rows : rows + pool, :].astype(bf16)


def serve(asked, neg_rows, table, slot_count):
    width, entities = table.shape
    rows = asked.shape[0] * slot_count
    pool = neg_rows.shape[1]
    part = 1024
    return pl.pallas_call(
        functools.partial(serve_kernel, slot_count),
        out_shape=(
            jax.ShapeDtypeStruct((rows, width), bf16),
            jax.ShapeDtypeStruct((pool, width), bf16),
        ),
        grid=(entities // part,),
        in_specs=[
            pl.BlockSpec(asked.shape, lambda i: (0, 0)),
            pl.BlockSpec(neg_rows.shape, lambda i: (0, 0)),
            pl.BlockSpec((width, part), lambda i: (0, i)),
        ],
        out_specs=(
            pl.BlockSpec((rows, width), lambda i: (0, 0)),
            pl.BlockSpec((pool, width), lambda i: (0, 0)),
        ),
        scratch_shapes=[pltpu.VMEM((rows + pool, width), f32), pltpu.VMEM((rows + pool, 1), i32)],
        compiler_params=params(40),
        cost_estimate=pl.CostEstimate(
            flops=2 * (rows + pool) * width * entities,
            bytes_accessed=2 * width * entities,
            transcendentals=0,
        ),
        name="serve",
    )(asked, neg_rows, table)


def softplus(x):
    return jnp.maximum(x, 0.0) + jnp.log1p(jnp.exp(-jnp.abs(x)))


def relations_kernel(ids_ref, type_ref, center_hbm, offset_hbm, shift_ref, size_ref,
                     center_tab, offset_tab, center_sum, offset_rows, sems):
    hops, queries = ids_ref.shape
    width, rels = center_tab.shape
    copies = [
        pltpu.make_async_copy(center_hbm, center_tab, sems.at[0]),
        pltpu.make_async_copy(offset_hbm, offset_tab, sems.at[1]),
    ]
    for copy in copies:
        copy.start()
    center_sum[...] = jnp.zeros_like(center_sum)
    offset_rows[...] = jnp.zeros_like(offset_rows)
    for copy in copies:
        copy.wait()

    def part(base, size):
        columns = pl.ds(base, size)
        count = jnp.zeros((size, queries), f32)
        hots = []
        for hop in range(hops):
            hot = jnp.where(iota((size, queries), 0) + base == ids_ref[hop : hop + 1, :], 1.0, 0.0)
            hots.append(hot.astype(bf16))
            count = count + jnp.where(type_ref[...] >= hop, hot, 0.0)
        center_sum[...] += dot(center_tab[:, columns], count.astype(bf16), 1, 0)
        for hop in range(hops):
            here = pl.ds(hop * queries, queries)
            offset_rows[:, here] += dot(offset_tab[:, columns], hots[hop], 1, 0)

    step = 1024

    def body(i, _):
        part(pl.multiple_of(i * step, step), step)
        return 0

    lax.fori_loop(0, rels // step, body, 0)
    if rels % step:
        part(rels // step * step, rels % step)
    shift_ref[...] = center_sum[...]
    total = jnp.zeros((width, queries), f32)
    for hop in range(hops):
        value = softplus(offset_rows[:, hop * queries : (hop + 1) * queries])
        total = total + jnp.where(type_ref[...] >= hop, value, 0.0)
    size_ref[...] = total


def relations(rel_ids, query_type, rel_center, rel_offset):
    hops, queries = rel_ids.shape
    width, rels = rel_center.shape
    return pl.pallas_call(
        relations_kernel,
        out_shape=(
            jax.ShapeDtypeStruct((width, queries), f32),
            jax.ShapeDtypeStruct((width, queries), f32),
        ),
        in_specs=[whole(), whole(), pl.BlockSpec(memory_space=pl.ANY),
                  pl.BlockSpec(memory_space=pl.ANY)],
        out_specs=(whole(), whole()),
        scratch_shapes=[
            pltpu.VMEM((width, rels), bf16),
            pltpu.VMEM((width, rels), bf16),
            pltpu.VMEM((width, queries), f32),
            pltpu.VMEM((width, hops * queries), f32),
            pltpu.SemaphoreType.DMA((2,)),
        ],
        compiler_params=params(48),
        cost_estimate=pl.CostEstimate(
            flops=2 * (hops + 1) * queries * width * rels,
            bytes_accessed=4 * width * rels,
            transcendentals=0,
        ),
        name="relations",
    )(rel_ids, query_type, rel_center, rel_offset)


def slope_terms(gap, size):
    square = gap * gap + scaled_eps
    inverse = lax.rsqrt(square)
    spread = square * inverse
    above = 1.0 + jnp.exp2(spread - size)
    slope = (1.0 - slope_weight * pl.reciprocal(above, approx=True)) * (gap * inverse)
    return spread, above, slope


def grads_kernel(slot_ref, back_ref, shift_ref, size_ref, p0, p1, p2, p3, slots_ref, pool_ref,
                 entity, spread_out, center, size, grads, slopes, dists, weights, pool_grad):
    width, queries = shift_ref.shape
    rows = back_ref.shape[0]
    pool = p0.shape[0]
    negatives = 4 * pool
    tiles = width // 8

    hot = one_hot(iota((rows, 2 * queries), 0) == slot_ref[...])
    picked = dot(back_ref[...], hot, 0, 0)
    center[...] = (picked[:, 0:queries] + shift_ref[...]) * log2e
    size[...] = size_ref[...] * log2e
    grads[:, queries:] = picked[:, queries:] * log2e
    blocks = jnp.concatenate([p0[...], p1[...], p2[...], p3[...]], axis=0)
    eye = one_hot(iota((negatives, negatives), 0) == iota((negatives, negatives), 1))
    columns = dot(blocks, eye, 0, 0) * log2e
    high = columns.astype(bf16)
    entity[:, 0:negatives] = high
    entity[:, negatives:] = (columns - high.astype(f32)).astype(bf16)
    pool_grad[...] = jnp.zeros_like(pool_grad)

    spread, above, slope = slope_terms(grads[:, queries:] - center[...], size[...])
    total = jnp.sum(spread + log_weight * jnp.log2(above), axis=0, keepdims=True) * dist_unit
    weight = (loss_scale * dist_scale) / (1.0 + jnp.exp(margin_gamma - total))
    slope = slope * weight
    grads[:, 0:queries] = -slope
    grads[:, queries:] = slope

    halves = [pl.ds(half * lanes, lanes) for half in range(queries // lanes)]
    lane = iota((8, lanes), 1)
    group = 4
    block = 10

    def chunk(j, _):
        here = j * near
        picks = iota((2 * negatives, near * lanes), 0) & (negatives - 1)
        picks = one_hot(picks == here + lax.shift_right_logical(iota(picks.shape, 1), 7))
        spread_out[...] = dot(entity[...], picks, 1, 0)
        for first in range(0, near, group):
            def forward(base, count, sums):
                sums = list(sums)
                for k in range(group):
                    at = first + k
                    for half, ql in enumerate(halves):
                        product = None
                        total = sums[half * group + k]
                        for tile in range(count):
                            d = pl.ds(base + tile * 8, 8)
                            column = spread_out[d, at * lanes : (at + 1) * lanes]
                            spread, above, slope = slope_terms(column - center[d, ql], size[d, ql])
                            slopes[at, d, ql] = slope
                            product = above if product is None else product * above
                            total = total + spread
                        sums[half * group + k] = total + log_weight * jnp.log2(product)
                return tuple(sums)

            sums = tuple(jnp.zeros((8, lanes), f32) for _ in range(group * len(halves)))
            sums = lax.fori_loop(
                0, tiles // 4, lambda i, s: forward(pl.multiple_of(i * 32, 32), 4, s), sums
            )
            if tiles % 4:
                sums = forward(tiles // 4 * 32, tiles % 4, sums)
            for half, ql in enumerate(halves):
                for k in range(group):
                    dists[first + k : first + k + 1, ql] = jnp.sum(
                        sums[half * group + k], axis=0, keepdims=True
                    )
        scale = -loss_scale * dist_scale / negatives
        weights[...] = scale / (1.0 + jnp.exp(dists[...] * dist_unit - margin_gamma))
        weight_rows = [
            [jnp.broadcast_to(weights[k : k + 1, ql], (8, lanes)) for ql in halves]
            for k in range(near)
        ]

        def backward(i, _):
            for tile in range(block):
                d = pl.ds(pl.multiple_of(i * (8 * block), 8) + tile * 8, 8)
                to_center = [grads[d, ql] for ql in halves]
                to_pool = pool_grad[d, :]
                for k in range(near):
                    row = None
                    for half, ql in enumerate(halves):
                        term = slopes[k, d, ql] * weight_rows[k][half]
                        to_center[half] = to_center[half] - term
                        row = term if row is None else row + term
                    row = jnp.sum(row, axis=1, keepdims=True)
                    to_pool = jnp.where(lane == here + k, row, to_pool)
                for half, ql in enumerate(halves):
                    grads[d, ql] = to_center[half]
                pool_grad[d, :] = to_pool
            return 0

        lax.fori_loop(0, tiles // block, backward, 0)
        return 0

    lax.fori_loop(0, negatives // near, chunk, 0)

    value = grads[...]
    high = value.astype(bf16)
    low = (value - high.astype(f32)).astype(bf16)
    slots_ref[...] = dot(hot, high, 1, 1) + dot(hot, low, 1, 1)
    pool_ref[...] = jnp.transpose(pool_grad[...])[:, 0:width]


def gradients(slot, back, shift, size, blocks):
    width, queries = shift.shape
    rows = back.shape[0]
    pool = blocks[0].shape[0]
    negatives = 4 * pool
    padded = -(-width // lanes) * lanes
    work = negatives * queries * width
    return pl.pallas_call(
        grads_kernel,
        out_shape=(
            jax.ShapeDtypeStruct((rows, width), f32),
            jax.ShapeDtypeStruct((negatives, width), f32),
        ),
        in_specs=[whole()] * 8,
        out_specs=(whole(), whole()),
        scratch_shapes=[
            pltpu.VMEM((width, 2 * negatives), bf16),
            pltpu.VMEM((width, near * lanes), f32),
            pltpu.VMEM((width, queries), f32),
            pltpu.VMEM((width, queries), f32),
            pltpu.VMEM((width, 2 * queries), f32),
            pltpu.VMEM((near, width, queries), f32),
            pltpu.VMEM((near, queries), f32),
            pltpu.VMEM((near, queries), f32),
            pltpu.VMEM((padded, negatives), f32),
        ],
        compiler_params=params(48),
        cost_estimate=pl.CostEstimate(
            flops=16 * work, bytes_accessed=4 * rows * width, transcendentals=3 * work
        ),
        name="gradients",
    )(slot, back, shift, size, *blocks)


def scatter_kernel(slot_count, asked_ref, neg_ref, back_ref, own_ref, q1, q2, q3, out_ref, column, both):
    step = pl.program_id(0)
    part = out_ref.shape[1]
    rows, width = back_ref.shape
    pool = q1.shape[0]

    @pl.when(step == 0)
    def _():
        column[0:rows, :] = asked_column(asked_ref[...], slot_count)
        here = iota((pool, pool), 0) == iota((pool, pool), 1)
        column[rows:, :] = jnp.sum(
            jnp.where(here, neg_ref[...].astype(f32), 0.0), axis=1, keepdims=True
        ).astype(i32)

        def place(value, start):
            size = value.shape[0]
            high = value.astype(bf16)
            low = (value - high.astype(f32)).astype(bf16)
            both[start : start + size, 0:width] = high
            both[start : start + size, 512 : 512 + width] = low

        both[...] = jnp.zeros_like(both)
        place(back_ref[...], 0)
        place(own_ref[...] + q1[...] + q2[...] + q3[...], rows)

    hot = one_hot(iota((rows + pool, part), 1) + step * part == column[...])
    result = dot(both[...], hot, 0, 0)
    out_ref[...] = result[0:width, :] + result[512 : 512 + width, :]


def scatter(asked, neg_rows, back, own, others, slot_count, entities):
    rows, width = back.shape
    pool = own.shape[0]
    part = 512
    fixed = lambda i: (0, 0)
    return pl.pallas_call(
        functools.partial(scatter_kernel, slot_count),
        out_shape=jax.ShapeDtypeStruct((width, entities), f32),
        grid=(entities // part,),
        in_specs=[
            pl.BlockSpec(asked.shape, fixed),
            pl.BlockSpec(neg_rows.shape, fixed),
            pl.BlockSpec((rows, width), fixed),
        ]
        + [pl.BlockSpec((pool, width), fixed)] * 4,
        out_specs=pl.BlockSpec((width, part), lambda i: (0, i)),
        scratch_shapes=[pltpu.VMEM((rows + pool, 1), i32), pltpu.VMEM((rows + pool, 1024), bf16)],
        compiler_params=params(48),
        name="scatter",
    )(asked, neg_rows, back, own, *others)


def local(
    entity_table, rel_center, rel_offset, entity_owner, entity_row, rel_ids, query_type, neg_rows
):
    entities, width = entity_table.shape
    table_size = lax.axis_size("table")
    group_size = lax.axis_size("blk")
    devices = table_size * group_size
    queries = rel_ids.shape[0]
    slot_count = 4 * queries // devices
    pool = neg_rows.shape[0]
    axes = ("table", "blk")
    exchange = functools.partial(
        lax.all_to_all, axis_name=axes, split_axis=0, concat_axis=0, tiled=True
    )
    table = entity_table.T
    neg_row = neg_rows.reshape(1, pool)
    wanted, slot = plan_slots(
        entity_owner[:, :, 0].T, entity_row.T, slot_count, devices
    )
    asked = exchange(wanted.reshape(devices, 1, lanes)).reshape(devices, lanes)
    served, block = serve(asked, neg_row, table, slot_count)
    back = exchange(served.reshape(devices, slot_count, width)).reshape(-1, width)
    shift, size = relations(rel_ids.T, query_type.reshape(1, queries), rel_center.T, rel_offset.T)
    blocks = [block] + [shifted(block, "blk", step) for step in range(1, group_size)]
    slot_grads, pool_grads = gradients(slot, back, shift, size, blocks)
    returned = exchange(slot_grads.reshape(devices, slot_count, width)).reshape(-1, width)
    others = [
        shifted(pool_grads[step * pool : (step + 1) * pool], "blk", -step)
        for step in range(1, group_size)
    ]
    return scatter(
        asked, neg_row, returned, pool_grads[0:pool], others, slot_count, entities
    ).T


def solution(mesh):
    placed = (
        P(("table", "blk"), None),
        P(),
        P(),
        P(("table", "blk"), None, None),
        P(("table", "blk"), None),
        P(("table", "blk"), None),
        P(("table", "blk")),
        P(("table", "blk")),
    )
    return jax.shard_map(
        local, mesh=mesh, in_specs=placed, out_specs=P(("table", "blk"), None), check_vma=False
    )
```

```python
import functools
import math
import jax
import jax.numpy as jnp
from jax import lax
from jax.experimental import pallas as pl
from jax.experimental.pallas import tpu as pltpu
from jax.sharding import PartitionSpec as P

margin_gamma = 7.0
dist_scale = 0.02
inside_weight = 0.2
smooth_eps = 0.01
loss_scale = 64.0

f32 = jnp.float32
bf16 = jnp.bfloat16
i32 = jnp.int32
log2e = math.log2(math.e)
scaled_eps = smooth_eps * log2e * log2e
dist_unit = dist_scale * math.log(2.0) * inside_weight
log_weight = (1.0 - inside_weight) / inside_weight
slope_weight = 1.0 - inside_weight
lanes = 128
near = 8


def iota(shape, axis):
    return lax.broadcasted_iota(i32, shape, axis)


def dot(a, b, ca, cb):
    return lax.dot_general(a, b, (((ca,), (cb,)), ((), ())), preferred_element_type=f32)


def whole():
    return pl.BlockSpec(memory_space=pltpu.VMEM)


def params(mib, **more):
    return pltpu.CompilerParams(vmem_limit_bytes=mib * 2**20, **more)


def shifted(value, axis, steps):
    count = lax.axis_size(axis)
    pairs = [(source, (source + steps) % count) for source in range(count)]
    return lax.ppermute(value, axis, pairs)


def one_hot(mask):
    return jnp.where(mask, 1.0, 0.0).astype(bf16)


def slots_kernel(slot_count, devices, owner_ref, row_ref, wanted_ref, slot_ref):
    owner = jnp.concatenate([owner_ref[0:1, :], owner_ref[1:2, :]], axis=1)
    row = jnp.concatenate([row_ref[0:1, :], row_ref[1:2, :]], axis=1)
    requests = owner.shape[1]
    named = iota((devices, requests), 0) == owner
    named_hot = one_hot(named)
    earlier = one_hot(iota((requests, requests), 0) < iota((requests, requests), 1))
    before = dot(named_hot, earlier, 1, 0)
    rank = jnp.sum(jnp.where(named, before, 0.0), axis=0, keepdims=True).astype(i32)
    slot_ref[...] = owner * slot_count + rank
    high = lax.shift_right_logical(row, 6)
    low = row - high * 64
    ranked = iota((lanes, requests), 0) == rank
    high_hot = jnp.where(ranked, high.astype(f32), 0.0).astype(bf16)
    low_hot = jnp.where(ranked, low.astype(f32), 0.0).astype(bf16)
    asked = dot(named_hot, high_hot, 1, 1) * 64.0 + dot(named_hot, low_hot, 1, 1)
    wanted_ref[...] = asked.astype(i32)


def plan_slots(owner, row, slot_count, devices):
    requests = owner.shape[0] * owner.shape[1]
    return pl.pallas_call(
        functools.partial(slots_kernel, slot_count, devices),
        out_shape=(
            jax.ShapeDtypeStruct((devices, lanes), i32),
            jax.ShapeDtypeStruct((1, requests), i32),
        ),
        in_specs=[whole(), whole()],
        out_specs=(whole(), whole()),
        compiler_params=params(32),
        name="plan_slots",
    )(owner, row)


def asked_column(asked, slot_count):
    devices = asked.shape[0]
    rows = devices * slot_count
    high = lax.shift_right_logical(asked, 6)
    low = asked - high * 64
    group = lax.shift_right_logical(iota((rows, devices), 0), int(math.log2(slot_count)))
    pick = one_hot(group == iota((rows, devices), 1))
    spread = dot(pick, high.astype(f32).astype(bf16), 1, 0) * 64.0 + dot(
        pick, low.astype(f32).astype(bf16), 1, 0
    )
    mine = (iota((rows, lanes), 0) & (slot_count - 1)) == iota((rows, lanes), 1)
    return jnp.sum(jnp.where(mine, spread, 0.0), axis=1, keepdims=True).astype(i32)


def serve_kernel(slot_count, asked_ref, neg_ref, table_ref, served_ref, pool_ref, total, column):
    step = pl.program_id(0)
    part = table_ref.shape[1]
    rows = served_ref.shape[0]
    pool = pool_ref.shape[0]

    @pl.when(step == 0)
    def _():
        column[0:rows, :] = asked_column(asked_ref[...], slot_count)
        here = iota((pool, pool), 0) == iota((pool, pool), 1)
        column[rows : rows + pool, :] = jnp.sum(
            jnp.where(here, neg_ref[...].astype(f32), 0.0), axis=1, keepdims=True
        ).astype(i32)
        total[...] = jnp.zeros_like(total)

    base = step * part
    for start in range(0, rows + pool, 256):
        size = min(256, rows + pool - start)
        block = pl.ds(start, size)
        hot = one_hot(iota((size, part), 1) + base == column[block, :])
        total[block, :] += dot(hot, table_ref[...], 1, 1)

    @pl.when(step == pl.num_programs(0) - 1)
    def _():
        served_ref[...] = total[0:rows, :].astype(bf16)
        pool_ref[...] = total[rows : rows + pool, :].astype(bf16)


def serve(asked, neg_rows, table, slot_count):
    width, entities = table.shape
    rows = asked.shape[0] * slot_count
    pool = neg_rows.shape[1]
    part = 1024
    return pl.pallas_call(
        functools.partial(serve_kernel, slot_count),
        out_shape=(
            jax.ShapeDtypeStruct((rows, width), bf16),
            jax.ShapeDtypeStruct((pool, width), bf16),
        ),
        grid=(entities // part,),
        in_specs=[
            pl.BlockSpec(asked.shape, lambda i: (0, 0)),
            pl.BlockSpec(neg_rows.shape, lambda i: (0, 0)),
            pl.BlockSpec((width, part), lambda i: (0, i)),
        ],
        out_specs=(
            pl.BlockSpec((rows, width), lambda i: (0, 0)),
            pl.BlockSpec((pool, width), lambda i: (0, 0)),
        ),
        scratch_shapes=[pltpu.VMEM((rows + pool, width), f32), pltpu.VMEM((rows + pool, 1), i32)],
        compiler_params=params(40),
        cost_estimate=pl.CostEstimate(
            flops=2 * (rows + pool) * width * entities,
            bytes_accessed=2 * width * entities,
            transcendentals=0,
        ),
        name="serve",
    )(asked, neg_rows, table)


def softplus(x):
    return jnp.maximum(x, 0.0) + jnp.log1p(jnp.exp(-jnp.abs(x)))


def relations_kernel(ids_ref, type_ref, center_hbm, offset_hbm, shift_ref, size_ref,
                     center_tab, offset_tab, center_sum, offset_rows, sems):
    hops, queries = ids_ref.shape
    width, rels = center_tab.shape
    copies = [
        pltpu.make_async_copy(center_hbm, center_tab, sems.at[0]),
        pltpu.make_async_copy(offset_hbm, offset_tab, sems.at[1]),
    ]
    for copy in copies:
        copy.start()
    center_sum[...] = jnp.zeros_like(center_sum)
    offset_rows[...] = jnp.zeros_like(offset_rows)
    for copy in copies:
        copy.wait()

    def part(base, size):
        columns = pl.ds(base, size)
        count = jnp.zeros((size, queries), f32)
        hots = []
        for hop in range(hops):
            hot = jnp.where(iota((size, queries), 0) + base == ids_ref[hop : hop + 1, :], 1.0, 0.0)
            hots.append(hot.astype(bf16))
            count = count + jnp.where(type_ref[...] >= hop, hot, 0.0)
        center_sum[...] += dot(center_tab[:, columns], count.astype(bf16), 1, 0)
        for hop in range(hops):
            here = pl.ds(hop * queries, queries)
            offset_rows[:, here] += dot(offset_tab[:, columns], hots[hop], 1, 0)

    step = 1024

    def body(i, _):
        part(pl.multiple_of(i * step, step), step)
        return 0

    lax.fori_loop(0, rels // step, body, 0)
    if rels % step:
        part(rels // step * step, rels % step)
    shift_ref[...] = center_sum[...]
    total = jnp.zeros((width, queries), f32)
    for hop in range(hops):
        value = softplus(offset_rows[:, hop * queries : (hop + 1) * queries])
        total = total + jnp.where(type_ref[...] >= hop, value, 0.0)
    size_ref[...] = total


def relations(rel_ids, query_type, rel_center, rel_offset):
    hops, queries = rel_ids.shape
    width, rels = rel_center.shape
    return pl.pallas_call(
        relations_kernel,
        out_shape=(
            jax.ShapeDtypeStruct((width, queries), f32),
            jax.ShapeDtypeStruct((width, queries), f32),
        ),
        in_specs=[whole(), whole(), pl.BlockSpec(memory_space=pl.ANY),
                  pl.BlockSpec(memory_space=pl.ANY)],
        out_specs=(whole(), whole()),
        scratch_shapes=[
            pltpu.VMEM((width, rels), bf16),
            pltpu.VMEM((width, rels), bf16),
            pltpu.VMEM((width, queries), f32),
            pltpu.VMEM((width, hops * queries), f32),
            pltpu.SemaphoreType.DMA((2,)),
        ],
        compiler_params=params(48),
        cost_estimate=pl.CostEstimate(
            flops=2 * (hops + 1) * queries * width * rels,
            bytes_accessed=4 * width * rels,
            transcendentals=0,
        ),
        name="relations",
    )(rel_ids, query_type, rel_center, rel_offset)


def slope_terms(gap, size):
    square = gap * gap + scaled_eps
    inverse = lax.rsqrt(square)
    spread = square * inverse
    above = 1.0 + jnp.exp2(spread - size)
    slope = (1.0 / slope_weight - pl.reciprocal(above, approx=True)) * (gap * inverse)
    return spread, above, slope


def grads_kernel(slot_ref, back_ref, shift_ref, size_ref, p0, p1, p2, p3, slots_ref, pool_ref,
                 entity, picks, spread_out, center, size, grads, slopes, dists, weights, pool_grad, codes):
    width, queries = shift_ref.shape
    rows = back_ref.shape[0]
    pool = p0.shape[0]
    negatives = 4 * pool
    tiles = width // 8

    hot = one_hot(iota((rows, 2 * queries), 0) == slot_ref[...])
    picked = dot(back_ref[...], hot, 0, 0)
    center[...] = (picked[:, 0:queries] + shift_ref[...]) * log2e
    size[...] = size_ref[...] * log2e
    grads[:, queries:] = picked[:, queries:] * log2e
    blocks = jnp.concatenate([p0[...], p1[...], p2[...], p3[...]], axis=0)
    eye = one_hot(iota((negatives, negatives), 0) == iota((negatives, negatives), 1))
    columns = dot(blocks, eye, 0, 0) * log2e
    high = columns.astype(bf16)
    entity[:, 0:negatives] = high
    entity[:, negatives:] = (columns - high.astype(f32)).astype(bf16)
    pool_grad[...] = jnp.zeros_like(pool_grad)

    spread, above, slope = slope_terms(grads[:, queries:] - center[...], size[...])
    total = jnp.sum(spread + log_weight * jnp.log2(above), axis=0, keepdims=True) * dist_unit
    weight = (loss_scale * dist_scale * slope_weight) / (1.0 + jnp.exp(margin_gamma - total))
    slope = slope * weight
    grads[:, 0:queries] = -slope
    grads[:, queries:] = slope

    halves = [pl.ds(half * lanes, lanes) for half in range(queries // lanes)]
    lane = iota((8, lanes), 1)
    group = 4
    reach = 50

    def pick(j):
        source = iota((2 * negatives, near * lanes), 0) & (negatives - 1)
        target = lax.shift_right_logical(iota(source.shape, 1), 7)
        return one_hot(source == j * near + target)

    spread_out[0] = dot(entity[...], pick(0), 1, 0)

    def chunk(j, _):
        here = j * near
        now = lax.rem(j, 2)
        for first in range(0, near, group):
            def forward(base, count, sums):
                sums = list(sums)
                for k in range(group):
                    at = first + k
                    for half, ql in enumerate(halves):
                        total = sums[half * group + k]
                        product = None
                        for tile in range(count):
                            d = pl.ds(base + tile * 8, 8)
                            column = spread_out[now, d, at * lanes : (at + 1) * lanes]
                            spread, above, slope = slope_terms(column - center[d, ql], size[d, ql])
                            slopes[at, d, ql] = slope
                            product = above if product is None else product * above
                            total = total + spread
                            if tile % 4 == 3 or tile == count - 1:
                                total = total + log_weight * jnp.log2(product)
                                product = None
                        sums[half * group + k] = total
                return tuple(sums)

            sums = tuple(jnp.zeros((8, lanes), f32) for _ in range(group * len(halves)))
            for start in range(0, tiles, reach):
                sums = forward(start * 8, min(reach, tiles - start), sums)
            for half, ql in enumerate(halves):
                for k in range(group):
                    dists[first + k : first + k + 1, ql] = jnp.sum(
                        sums[half * group + k], axis=0, keepdims=True
                    )
        scale = -loss_scale * dist_scale * slope_weight / negatives
        weights[...] = scale / (1.0 + jnp.exp(dists[...] * dist_unit - margin_gamma))
        weight_rows = [
            [jnp.broadcast_to(weights[k : k + 1, ql], (8, lanes)) for ql in halves]
            for k in range(near)
        ]

        picks[...] = pick(j + 1)

        spread_out[1 - now] = dot(entity[...], picks[...], 1, 0)
        for tile in range(tiles):
            d = pl.ds(tile * 8, 8)
            to_center = [grads[d, ql] for ql in halves]
            to_pool = pool_grad[d, :]
            for k in range(near):
                row = None
                for half, ql in enumerate(halves):
                    term = slopes[k, d, ql] * weight_rows[k][half]
                    to_center[half] = to_center[half] - term
                    row = term if row is None else row + term
                row = jnp.sum(row, axis=1, keepdims=True)
                to_pool = jnp.where(lane == here + k, row, to_pool)
            for half, ql in enumerate(halves):
                grads[d, ql] = to_center[half]
            pool_grad[d, :] = to_pool
        return 0

    lax.fori_loop(0, negatives // near, chunk, 0)

    value = grads[...]
    most = jnp.max(jnp.abs(value), axis=0, keepdims=True)
    power = 14.0 - jnp.floor(jnp.log2(jnp.maximum(most, 1e-30)))
    level = jnp.minimum(jnp.maximum(jnp.round(value * jnp.exp2(power)), -32767.0), 32767.0)
    high = jnp.floor(level * (1.0 / 256.0) + 0.5)
    low = level - high * 256.0
    codes[...] = jnp.zeros_like(codes)
    codes[0:width, 0 : 2 * queries] = high.astype(bf16)
    codes[0:width, 2 * queries :] = low.astype(bf16)
    codes[width : width + 16, 2 * queries :] = jnp.broadcast_to(power, (16, 2 * queries)).astype(bf16)
    level = dot(hot, codes[:, 0 : 2 * queries], 1, 1) * 256.0 + dot(hot, codes[:, 2 * queries :], 1, 1)
    slots_ref[...] = level.astype(i32).astype(jnp.int16)
    pool_ref[...] = jnp.transpose(pool_grad[...])[:, 0:width]


def gradients(slot, back, shift, size, blocks):
    width, queries = shift.shape
    rows = back.shape[0]
    pool = blocks[0].shape[0]
    negatives = 4 * pool
    padded = -(-width // lanes) * lanes
    work = negatives * queries * width
    return pl.pallas_call(
        grads_kernel,
        out_shape=(
            jax.ShapeDtypeStruct((rows, padded), jnp.int16),
            jax.ShapeDtypeStruct((negatives, width), f32),
        ),
        in_specs=[whole()] * 8,
        out_specs=(whole(), whole()),
        scratch_shapes=[
            pltpu.VMEM((width, 2 * negatives), bf16),
            pltpu.VMEM((2 * negatives, near * lanes), bf16),
            pltpu.VMEM((2, width, near * lanes), f32),
            pltpu.VMEM((width, queries), f32),
            pltpu.VMEM((width, queries), f32),
            pltpu.VMEM((width, 2 * queries), f32),
            pltpu.VMEM((near, width, queries), f32),
            pltpu.VMEM((near, queries), f32),
            pltpu.VMEM((near, queries), f32),
            pltpu.VMEM((padded, negatives), f32),
            pltpu.VMEM((padded, 4 * queries), bf16),
        ],
        compiler_params=params(48),
        cost_estimate=pl.CostEstimate(
            flops=16 * work, bytes_accessed=4 * rows * width, transcendentals=3 * work
        ),
        name="gradients",
    )(slot, back, shift, size, *blocks)


def scatter_kernel(slot_count, asked_ref, neg_ref, back_ref, own_ref, q1, q2, q3, out_ref, column, rows_of, both):
    step = pl.program_id(0)
    width, part = out_ref.shape
    rows, padded = back_ref.shape
    pool = q1.shape[0]

    @pl.when(step == 0)
    def _():
        column[0:rows, :] = asked_column(asked_ref[...], slot_count)
        here = iota((pool, pool), 0) == iota((pool, pool), 1)
        column[rows : rows + pool, :] = jnp.sum(
            jnp.where(here, neg_ref[...].astype(f32), 0.0), axis=1, keepdims=True
        ).astype(i32)
        column[rows + pool :, :] = jnp.full((lanes - pool, 1), -1, i32)
        level = back_ref[...].astype(i32).astype(f32)
        rows_of[0:rows, :] = level * jnp.exp2(-level[:, width : width + 1])
        rows_of[rows:, :] = jnp.zeros((lanes, padded), f32)
        rows_of[rows : rows + pool, 0:width] = own_ref[...] + q1[...] + q2[...] + q3[...]
        value = jnp.transpose(rows_of[...])[0:width, :]
        high = value.astype(bf16)
        both[0:width, :] = high
        both[width:, :] = (value - high.astype(f32)).astype(bf16)

    hot = one_hot(iota((rows + lanes, part), 1) + step * part == column[...])
    result = dot(both[...], hot, 1, 0)
    out_ref[...] = result[0:width, :] + result[width:, :]


def scatter(asked, neg_rows, back, own, others, slot_count, entities):
    rows, padded = back.shape
    pool, width = own.shape
    part = 512
    fixed = lambda i: (0, 0)
    return pl.pallas_call(
        functools.partial(scatter_kernel, slot_count),
        out_shape=jax.ShapeDtypeStruct((width, entities), f32),
        grid=(entities // part,),
        in_specs=[
            pl.BlockSpec(asked.shape, fixed),
            pl.BlockSpec(neg_rows.shape, fixed),
            pl.BlockSpec((rows, padded), fixed),
        ]
        + [pl.BlockSpec((pool, width), fixed)] * 4,
        out_specs=pl.BlockSpec((width, part), lambda i: (0, i)),
        scratch_shapes=[
            pltpu.VMEM((rows + lanes, 1), i32),
            pltpu.VMEM((rows + lanes, padded), f32),
            pltpu.VMEM((2 * width, rows + lanes), bf16),
        ],
        compiler_params=params(48),
        name="scatter",
    )(asked, neg_rows, back, own, *others)


def local(
    entity_table, rel_center, rel_offset, entity_owner, entity_row, rel_ids, query_type, neg_rows
):
    entities, width = entity_table.shape
    table_size = lax.axis_size("table")
    group_size = lax.axis_size("blk")
    devices = table_size * group_size
    queries = rel_ids.shape[0]
    slot_count = 4 * queries // devices
    pool = neg_rows.shape[0]
    axes = ("table", "blk")
    exchange = functools.partial(
        lax.all_to_all, axis_name=axes, split_axis=0, concat_axis=0, tiled=True
    )
    table = entity_table.T
    neg_row = neg_rows.reshape(1, pool)
    wanted, slot = plan_slots(
        entity_owner[:, :, 0].T, entity_row.T, slot_count, devices
    )
    asked = exchange(wanted.reshape(devices, 1, lanes)).reshape(devices, lanes)
    served, block = serve(asked, neg_row, table, slot_count)
    back = exchange(served.reshape(devices, slot_count, width)).reshape(-1, width)
    shift, size = relations(rel_ids.T, query_type.reshape(1, queries), rel_center.T, rel_offset.T)
    blocks = [block] + [shifted(block, "blk", step) for step in range(1, group_size)]
    slot_grads, pool_grads = gradients(slot, back, shift, size, blocks)
    padded = slot_grads.shape[1]
    returned = exchange(slot_grads.reshape(devices, slot_count, padded)).reshape(-1, padded)
    others = [
        shifted(pool_grads[step * pool : (step + 1) * pool], "blk", -step)
        for step in range(1, group_size)
    ]
    return scatter(
        asked, neg_row, returned, pool_grads[0:pool], others, slot_count, entities
    ).T


def solution(mesh):
    placed = (
        P(("table", "blk"), None),
        P(),
        P(),
        P(("table", "blk"), None, None),
        P(("table", "blk"), None),
        P(("table", "blk"), None),
        P(("table", "blk")),
        P(("table", "blk")),
    )
    return jax.shard_map(
        local, mesh=mesh, in_specs=placed, out_specs=P(("table", "blk"), None), check_vma=False
    )
```

```python
import functools
import math
import jax
import jax.numpy as jnp
from jax import lax
from jax.experimental import pallas as pl
from jax.experimental.pallas import tpu as pltpu
from jax.sharding import PartitionSpec as P

margin_gamma = 7.0
dist_scale = 0.02
inside_weight = 0.2
smooth_eps = 0.01
loss_scale = 64.0

f32 = jnp.float32
bf16 = jnp.bfloat16
i32 = jnp.int32
log2e = math.log2(math.e)
scaled_eps = smooth_eps * log2e * log2e
dist_unit = dist_scale * math.log(2.0) * inside_weight
log_weight = (1.0 - inside_weight) / inside_weight
slope_weight = 1.0 - inside_weight
lanes = 128
MESH = pl.DeviceIdType.MESH
near = 8


def iota(shape, axis):
    return lax.broadcasted_iota(i32, shape, axis)


def dot(a, b, ca, cb):
    return lax.dot_general(a, b, (((ca,), (cb,)), ((), ())), preferred_element_type=f32)


def whole():
    return pl.BlockSpec(memory_space=pltpu.VMEM)


def params(mib, **more):
    return pltpu.CompilerParams(vmem_limit_bytes=mib * 2**20, **more)


def shifted(value, axis, steps):
    count = lax.axis_size(axis)
    pairs = [(source, (source + steps) % count) for source in range(count)]
    return lax.ppermute(value, axis, pairs)


def one_hot(mask):
    return jnp.where(mask, 1.0, 0.0).astype(bf16)


def plan_slots(owner_ref, row_ref, slot_count, devices, mates):
    owner = jnp.concatenate([owner_ref[0:1, :], owner_ref[1:2, :]], axis=1)
    row = jnp.concatenate([row_ref[0:1, :], row_ref[1:2, :]], axis=1)
    requests = owner.shape[1]
    bits = int(math.log2(mates))
    place = (owner & (mates - 1)) * (devices // mates) + lax.shift_right_logical(owner, bits)
    named = iota((devices, requests), 0) == place
    named_hot = one_hot(named)
    earlier = one_hot(iota((requests, requests), 0) < iota((requests, requests), 1))
    before = dot(named_hot, earlier, 1, 0)
    rank = jnp.sum(jnp.where(named, before, 0.0), axis=0, keepdims=True).astype(i32)
    high = lax.shift_right_logical(row, 6)
    low = row - high * 64
    lane = iota((lanes, requests), 0)
    parts = jnp.where(lane == rank, high.astype(f32), 0.0)
    parts = parts + jnp.where(lane == rank + slot_count, low.astype(f32), 0.0)
    return owner * slot_count + rank, dot(named_hot, parts.astype(bf16), 1, 1)


def asked_column(asked, slot_count):
    devices = asked.shape[0]
    rows = devices * slot_count
    group = lax.shift_right_logical(iota((rows, devices), 0), int(math.log2(slot_count)))
    pick = one_hot(group == iota((rows, devices), 1))
    spread = dot(pick, asked.astype(bf16), 1, 0)
    slot = iota((rows, lanes), 0) & (slot_count - 1)
    lane = iota((rows, lanes), 1)
    row = jnp.where(lane == slot, spread * 64.0, jnp.where(lane == slot + slot_count, spread, 0.0))
    return jnp.sum(row, axis=1, keepdims=True).astype(i32)


def column_of(row):
    size = row.shape[1]
    here = iota((size, size), 0) == iota((size, size), 1)
    return jnp.sum(jnp.where(here, row.astype(f32), 0.0), axis=1, keepdims=True).astype(i32)


def softplus(x):
    return jnp.maximum(x, 0.0) + jnp.log1p(jnp.exp(-jnp.abs(x)))


def fetch_kernel(
    slot_count, table_size, group_size,
    owner_ref, row_ref, neg_ref, ids_ref, type_ref, table_hbm, center_hbm, offset_hbm,
    slot_ref, asked_ref, back_ref, block_ref, shift_ref, size_ref,
    table, center_tab, offset_tab, center_sum, offset_rows, wanted, passed, ordered, served, column,
    load_sems, first_send, first_recv, second_send, second_recv, row_send, row_recv,
    pool_send, pool_recv,
):
    hops, queries = ids_ref.shape
    width, rels = center_tab.shape
    entities = table.shape[1]
    devices = table_size * group_size
    mates = 2 * group_size
    teams = devices // mates
    row_me, col_me = lax.axis_index("table"), lax.axis_index("blk")
    me = row_me * group_size + col_me
    mate, team = lax.rem(me, mates), lax.div(me, mates)

    def target(index):
        return (lax.div(index, group_size), lax.rem(index, group_size))

    loads = [
        pltpu.make_async_copy(source, place, load_sems.at[i])
        for i, (source, place) in enumerate(
            [(table_hbm, table), (center_hbm, center_tab), (offset_hbm, offset_tab)]
        )
    ]
    for load in loads:
        load.start()

    barrier = pltpu.get_barrier_semaphore()

    def greet(i, _):
        pl.semaphore_signal(
            barrier, inc=1, device_id=target(lax.rem(me + i, devices)), device_id_type=MESH
        )
        return 0

    lax.fori_loop(1, devices, greet, 0)

    slot, asked = plan_slots(owner_ref, row_ref, slot_count, devices, mates)
    slot_ref[...] = slot
    wanted[...] = asked.reshape(mates, teams, lanes)
    center_sum[...] = jnp.zeros_like(center_sum)
    offset_rows[...] = jnp.zeros_like(offset_rows)

    pl.semaphore_wait(barrier, devices - 1)

    def first_hop(i, _):
        other = lax.rem(mate + i, mates)
        pltpu.make_async_remote_copy(
            src_ref=wanted.at[other], dst_ref=passed.at[mate],
            send_sem=first_send, recv_sem=first_recv,
            device_id=target(team * mates + other), device_id_type=MESH,
        ).start()
        return 0

    lax.fori_loop(1, mates, first_hop, 0)

    loads[0].wait()

    def rows_at(rows):
        total = None
        for start in range(0, entities, 1024):
            hot = one_hot(iota((rows.shape[0], 1024), 1) + start == rows)
            part = dot(hot, table[:, start : start + 1024], 1, 1)
            total = part if total is None else total + part
        return total.astype(bf16)

    block_ref[0] = rows_at(column_of(neg_ref[...]))
    pool_copies = []
    for step in range(1, group_size):
        copy = pltpu.make_async_remote_copy(
            src_ref=block_ref.at[0], dst_ref=block_ref.at[step],
            send_sem=pool_send.at[step], recv_sem=pool_recv.at[step],
            device_id=(row_me, lax.rem(col_me + step, group_size)), device_id_type=MESH,
        )
        copy.start()
        pool_copies.append(copy)

    def await_all(ref, count, sem):
        part = ref.at[pl.ds(0, count)]
        pltpu.make_async_copy(part, part, sem).wait()

    def relations(base, size):
        columns = pl.ds(base, size)
        count = jnp.zeros((size, queries), f32)
        hots = []
        for hop in range(hops):
            hot = jnp.where(iota((size, queries), 0) + base == ids_ref[hop : hop + 1, :], 1.0, 0.0)
            hots.append(hot.astype(bf16))
            count = count + jnp.where(type_ref[...] >= hop, hot, 0.0)
        center_sum[...] += dot(center_tab[:, columns], count.astype(bf16), 1, 0)
        for hop in range(hops):
            here = pl.ds(hop * queries, queries)
            offset_rows[:, here] += dot(offset_tab[:, columns], hots[hop], 1, 0)

    step = 1024
    whole_steps = rels // step
    cuts = (0, 2, 4, whole_steps)

    def relations_part(i):
        def body(k, _):
            relations(pl.multiple_of(k * step, step), step)
            return 0

        lax.fori_loop(cuts[i], cuts[i + 1], body, 0)

    passed[mate] = wanted[mate]
    await_all(wanted, mates - 1, first_send)
    await_all(passed, mates - 1, first_recv)
    source, target_row = iota((devices, devices), 1), iota((devices, devices), 0)
    mate_bits, team_bits = int(math.log2(mates)), int(math.log2(teams))
    order = one_hot(
        (target_row & (mates - 1)) * teams + lax.shift_right_logical(target_row, mate_bits) == source
    )
    ordered[...] = dot(order, passed[...].reshape(devices, lanes).astype(bf16), 1, 0).reshape(
        teams, mates, lanes
    )

    def second_hop(i, _):
        other = lax.rem(team + i, teams)
        pltpu.make_async_remote_copy(
            src_ref=ordered.at[other], dst_ref=asked_ref.at[team],
            send_sem=second_send, recv_sem=second_recv,
            device_id=target(other * mates + mate), device_id_type=MESH,
        ).start()
        return 0

    lax.fori_loop(1, teams, second_hop, 0)
    loads[1].wait()
    loads[2].wait()
    relations_part(0)
    asked_ref[team] = ordered[team]
    await_all(ordered, teams - 1, second_send)
    await_all(asked_ref, teams - 1, second_recv)

    column[...] = asked_column(asked_ref[...].reshape(devices, lanes), slot_count)
    quarter = devices // 4
    mine, inside = lax.div(me, quarter), lax.rem(me, quarter)
    for turn in (1, 2, 3, 0):
        part = lax.rem(mine + turn, 4)
        size = quarter * slot_count
        rows = rows_at(column[pl.ds(pl.multiple_of(part * size, size), size), :])
        served[pl.ds(part * quarter, quarter)] = rows.reshape(quarter, slot_count, width)

        def send_rows(i, _):
            other = part * quarter + lax.rem(inside + i, quarter)
            pltpu.make_async_remote_copy(
                src_ref=served.at[other], dst_ref=back_ref.at[me],
                send_sem=row_send, recv_sem=row_recv,
                device_id=target(other), device_id_type=MESH,
            ).start()
            return 0

        lax.fori_loop(1 if turn == 0 else 0, quarter, send_rows, 0)

    back_ref[me] = served[me]
    relations_part(1)
    relations_part(2)
    if rels % step:
        relations(whole_steps * step, rels % step)
    shift_ref[...] = center_sum[...]
    total = jnp.zeros((width, queries), f32)
    for hop in range(hops):
        value = softplus(offset_rows[:, hop * queries : (hop + 1) * queries])
        total = total + jnp.where(type_ref[...] >= hop, value, 0.0)
    size_ref[...] = total
    for copy in pool_copies:
        copy.wait()
    await_all(served, devices - 1, row_send)
    await_all(back_ref, devices - 1, row_recv)


def fetch(owner, row, neg_row, rel_ids, query_type, table, rel_center, rel_offset, slot_count,
          table_size, group_size):
    hops, queries = rel_ids.shape
    width, rels = rel_center.shape
    entities = table.shape[1]
    devices = table_size * group_size
    mates = 2 * group_size
    teams = devices // mates
    pool = neg_row.shape[1]
    anywhere = pl.BlockSpec(memory_space=pl.ANY)
    dma = pltpu.SemaphoreType.DMA
    return pl.pallas_call(
        functools.partial(fetch_kernel, slot_count, table_size, group_size),
        out_shape=(
            jax.ShapeDtypeStruct((1, 2 * queries), i32),
            jax.ShapeDtypeStruct((teams, mates, lanes), f32),
            jax.ShapeDtypeStruct((devices, slot_count, width), bf16),
            jax.ShapeDtypeStruct((group_size, pool, width), bf16),
            jax.ShapeDtypeStruct((width, queries), f32),
            jax.ShapeDtypeStruct((width, queries), f32),
        ),
        in_specs=[whole()] * 5 + [anywhere] * 3,
        out_specs=(whole(),) * 6,
        scratch_shapes=[
            pltpu.VMEM((width, entities), bf16),
            pltpu.VMEM((width, rels), bf16),
            pltpu.VMEM((width, rels), bf16),
            pltpu.VMEM((width, queries), f32),
            pltpu.VMEM((width, hops * queries), f32),
            pltpu.VMEM((mates, teams, lanes), f32),
            pltpu.VMEM((mates, teams, lanes), f32),
            pltpu.VMEM((teams, mates, lanes), f32),
            pltpu.VMEM((devices, slot_count, width), bf16),
            pltpu.VMEM((devices * slot_count, 1), i32),
            dma((3,)), dma, dma, dma, dma, dma, dma, dma((group_size,)), dma((group_size,)),
        ],
        compiler_params=params(52, collective_id=0, has_side_effects=True),
        name="fetch",
    )(owner, row, neg_row, rel_ids, query_type, table, rel_center, rel_offset)


def slope_terms(gap, size):
    square = gap * gap + scaled_eps
    inverse = lax.rsqrt(square)
    spread = square * inverse
    above = 1.0 + jnp.exp2(spread - size)
    slope = (1.0 / slope_weight - pl.reciprocal(above, approx=True)) * (gap * inverse)
    return spread, above, slope


def grads_kernel(slot_ref, back_ref, shift_ref, size_ref, block_ref, slots_ref, pool_ref,
                 entity, picks, spread_out, center, size, grads, slopes, dists, weights, pool_grad, codes):
    width, queries = shift_ref.shape
    rows = back_ref.shape[0]
    negatives = block_ref.shape[0]
    tiles = width // 8

    hot = one_hot(iota((rows, 2 * queries), 0) == slot_ref[...])
    picked = dot(back_ref[...], hot, 0, 0)
    center[...] = (picked[:, 0:queries] + shift_ref[...]) * log2e
    size[...] = size_ref[...] * log2e
    grads[:, queries:] = picked[:, queries:] * log2e
    eye = one_hot(iota((negatives, negatives), 0) == iota((negatives, negatives), 1))
    columns = dot(block_ref[...], eye, 0, 0) * log2e
    high = columns.astype(bf16)
    entity[:, 0:negatives] = high
    entity[:, negatives:] = (columns - high.astype(f32)).astype(bf16)
    pool_grad[...] = jnp.zeros_like(pool_grad)

    spread, above, slope = slope_terms(grads[:, queries:] - center[...], size[...])
    total = jnp.sum(spread + log_weight * jnp.log2(above), axis=0, keepdims=True) * dist_unit
    weight = (loss_scale * dist_scale * slope_weight) / (1.0 + jnp.exp(margin_gamma - total))
    slope = slope * weight
    grads[:, 0:queries] = -slope
    grads[:, queries:] = slope

    halves = [pl.ds(half * lanes, lanes) for half in range(queries // lanes)]
    lane = iota((8, lanes), 1)
    group = 4
    reach = 50

    def pick(j):
        source = iota((2 * negatives, near * lanes), 0) & (negatives - 1)
        target = lax.shift_right_logical(iota(source.shape, 1), 7)
        return one_hot(source == j * near + target)

    spread_out[0] = dot(entity[...], pick(0), 1, 0)

    def chunk(j, _):
        here = j * near
        now = lax.rem(j, 2)
        for first in range(0, near, group):
            def forward(base, count, sums):
                sums = list(sums)
                for k in range(group):
                    at = first + k
                    for half, ql in enumerate(halves):
                        total = sums[half * group + k]
                        product = None
                        for tile in range(count):
                            d = pl.ds(base + tile * 8, 8)
                            column = spread_out[now, d, at * lanes : (at + 1) * lanes]
                            spread, above, slope = slope_terms(column - center[d, ql], size[d, ql])
                            slopes[at, d, ql] = slope
                            product = above if product is None else product * above
                            total = total + spread
                            if tile % 4 == 3 or tile == count - 1:
                                total = total + log_weight * jnp.log2(product)
                                product = None
                        sums[half * group + k] = total
                return tuple(sums)

            sums = tuple(jnp.zeros((8, lanes), f32) for _ in range(group * len(halves)))
            for start in range(0, tiles, reach):
                sums = forward(start * 8, min(reach, tiles - start), sums)
            for half, ql in enumerate(halves):
                for k in range(group):
                    dists[first + k : first + k + 1, ql] = jnp.sum(
                        sums[half * group + k], axis=0, keepdims=True
                    )
        scale = -loss_scale * dist_scale * slope_weight / negatives
        weights[...] = scale / (1.0 + jnp.exp(dists[...] * dist_unit - margin_gamma))
        weight_rows = [
            [jnp.broadcast_to(weights[k : k + 1, ql], (8, lanes)) for ql in halves]
            for k in range(near)
        ]

        picks[...] = pick(j + 1)

        spread_out[1 - now] = dot(entity[...], picks[...], 1, 0)
        for tile in range(tiles):
            d = pl.ds(tile * 8, 8)
            to_center = [grads[d, ql] for ql in halves]
            to_pool = pool_grad[d, :]
            for k in range(near):
                row = None
                for half, ql in enumerate(halves):
                    term = slopes[k, d, ql] * weight_rows[k][half]
                    to_center[half] = to_center[half] - term
                    row = term if row is None else row + term
                row = jnp.sum(row, axis=1, keepdims=True)
                to_pool = jnp.where(lane == here + k, row, to_pool)
            for half, ql in enumerate(halves):
                grads[d, ql] = to_center[half]
            pool_grad[d, :] = to_pool
        return 0

    lax.fori_loop(0, negatives // near, chunk, 0)

    value = grads[...]
    most = jnp.max(jnp.abs(value), axis=0, keepdims=True)
    power = 14.0 - jnp.floor(jnp.log2(jnp.maximum(most, 1e-30)))
    level = jnp.minimum(jnp.maximum(jnp.round(value * jnp.exp2(power)), -32767.0), 32767.0)
    high = jnp.floor(level * (1.0 / 256.0) + 0.5)
    low = level - high * 256.0
    codes[...] = jnp.zeros_like(codes)
    codes[0:width, 0 : 2 * queries] = high.astype(bf16)
    codes[0:width, 2 * queries :] = low.astype(bf16)
    codes[width : width + 16, 2 * queries :] = jnp.broadcast_to(power, (16, 2 * queries)).astype(bf16)
    level = dot(hot, codes[:, 0 : 2 * queries], 1, 1) * 256.0 + dot(hot, codes[:, 2 * queries :], 1, 1)
    slots_ref[...] = level.astype(i32).astype(jnp.int16)
    pool_ref[...] = jnp.transpose(pool_grad[...])[:, 0:width]


def gradients(slot, back, shift, size, blocks):
    width, queries = shift.shape
    rows = back.shape[0]
    negatives = blocks.shape[0]
    padded = -(-width // lanes) * lanes
    work = negatives * queries * width
    return pl.pallas_call(
        grads_kernel,
        out_shape=(
            jax.ShapeDtypeStruct((rows, padded), jnp.int16),
            jax.ShapeDtypeStruct((negatives, width), f32),
        ),
        in_specs=[whole()] * 5,
        out_specs=(whole(), whole()),
        scratch_shapes=[
            pltpu.VMEM((width, 2 * negatives), bf16),
            pltpu.VMEM((2 * negatives, near * lanes), bf16),
            pltpu.VMEM((2, width, near * lanes), f32),
            pltpu.VMEM((width, queries), f32),
            pltpu.VMEM((width, queries), f32),
            pltpu.VMEM((width, 2 * queries), f32),
            pltpu.VMEM((near, width, queries), f32),
            pltpu.VMEM((near, queries), f32),
            pltpu.VMEM((near, queries), f32),
            pltpu.VMEM((padded, negatives), f32),
            pltpu.VMEM((padded, 4 * queries), bf16),
        ],
        compiler_params=params(48),
        cost_estimate=pl.CostEstimate(
            flops=16 * work, bytes_accessed=4 * rows * width, transcendentals=3 * work
        ),
        name="gradients",
    )(slot, back, shift, size, blocks)


def scatter_kernel(slot_count, asked_ref, neg_ref, back_ref, own_ref, q1, q2, q3, out_ref, column, rows_of, both):
    step = pl.program_id(0)
    width, part = out_ref.shape
    rows, padded = back_ref.shape
    pool = q1.shape[0]

    @pl.when(step == 0)
    def _():
        column[0:rows, :] = asked_column(asked_ref[...], slot_count)
        column[rows : rows + pool, :] = column_of(neg_ref[...])
        column[rows + pool :, :] = jnp.full((lanes - pool, 1), -1, i32)
        level = back_ref[...].astype(i32).astype(f32)
        rows_of[0:rows, :] = level * jnp.exp2(-level[:, width : width + 1])
        rows_of[rows:, :] = jnp.zeros((lanes, padded), f32)
        rows_of[rows : rows + pool, 0:width] = own_ref[...] + q1[...] + q2[...] + q3[...]
        value = jnp.transpose(rows_of[...])[0:width, :]
        high = value.astype(bf16)
        both[0:width, :] = high
        both[width:, :] = (value - high.astype(f32)).astype(bf16)

    hot = one_hot(iota((rows + lanes, part), 1) + step * part == column[...])
    result = dot(both[...], hot, 1, 0)
    out_ref[...] = result[0:width, :] + result[width:, :]


def scatter(asked, neg_rows, back, own, others, slot_count, entities):
    rows, padded = back.shape
    pool, width = own.shape
    part = 512
    fixed = lambda i: (0, 0)
    return pl.pallas_call(
        functools.partial(scatter_kernel, slot_count),
        out_shape=jax.ShapeDtypeStruct((width, entities), f32),
        grid=(entities // part,),
        in_specs=[
            pl.BlockSpec(asked.shape, fixed),
            pl.BlockSpec(neg_rows.shape, fixed),
            pl.BlockSpec((rows, padded), fixed),
        ]
        + [pl.BlockSpec((pool, width), fixed)] * 4,
        out_specs=pl.BlockSpec((width, part), lambda i: (0, i)),
        scratch_shapes=[
            pltpu.VMEM((rows + lanes, 1), i32),
            pltpu.VMEM((rows + lanes, padded), f32),
            pltpu.VMEM((2 * width, rows + lanes), bf16),
        ],
        compiler_params=params(48),
        name="scatter",
    )(asked, neg_rows, back, own, *others)


def local(
    entity_table, rel_center, rel_offset, entity_owner, entity_row, rel_ids, query_type, neg_rows
):
    entities, width = entity_table.shape
    table_size = lax.axis_size("table")
    group_size = lax.axis_size("blk")
    devices = table_size * group_size
    queries = rel_ids.shape[0]
    slot_count = 4 * queries // devices
    pool = neg_rows.shape[0]
    axes = ("table", "blk")
    exchange = functools.partial(
        lax.all_to_all, axis_name=axes, split_axis=0, concat_axis=0, tiled=True
    )
    table = entity_table.T
    neg_row = neg_rows.reshape(1, pool)
    slot, asked, back, blocks, shift, size = fetch(
        entity_owner[:, :, 0].T, entity_row.T, neg_row, rel_ids.T, query_type.reshape(1, queries),
        table, rel_center.T, rel_offset.T, slot_count, table_size, group_size,
    )
    asked = asked.reshape(devices, lanes)
    slot_grads, pool_grads = gradients(
        slot, back.reshape(-1, width), shift, size, blocks.reshape(-1, width)
    )
    padded = slot_grads.shape[1]
    returned = exchange(slot_grads.reshape(devices, slot_count, padded)).reshape(-1, padded)
    others = [
        shifted(pool_grads[step * pool : (step + 1) * pool], "blk", -step)
        for step in range(1, group_size)
    ]
    return scatter(
        asked, neg_row, returned, pool_grads[0:pool], others, slot_count, entities
    ).T


def solution(mesh):
    placed = (
        P(("table", "blk"), None),
        P(),
        P(),
        P(("table", "blk"), None, None),
        P(("table", "blk"), None),
        P(("table", "blk"), None),
        P(("table", "blk")),
        P(("table", "blk")),
    )
    return jax.shard_map(
        local, mesh=mesh, in_specs=placed, out_specs=P(("table", "blk"), None), check_vma=False
    )
```

```python
import functools
import math
import jax
import jax.numpy as jnp
from jax import lax
from jax.experimental import pallas as pl
from jax.experimental.pallas import tpu as pltpu
from jax.sharding import PartitionSpec as P

margin_gamma = 7.0
dist_scale = 0.02
inside_weight = 0.2
smooth_eps = 0.01
loss_scale = 64.0

f32 = jnp.float32
bf16 = jnp.bfloat16
i32 = jnp.int32
log2e = math.log2(math.e)
scaled_eps = smooth_eps * log2e * log2e
dist_unit = dist_scale * math.log(2.0) * inside_weight
log_weight = (1.0 - inside_weight) / inside_weight
slope_weight = 1.0 - inside_weight
lanes = 128
MESH = pl.DeviceIdType.MESH
near = 8


def iota(shape, axis):
    return lax.broadcasted_iota(i32, shape, axis)


def dot(a, b, ca, cb):
    return lax.dot_general(a, b, (((ca,), (cb,)), ((), ())), preferred_element_type=f32)


def whole():
    return pl.BlockSpec(memory_space=pltpu.VMEM)


def params(mib, **more):
    return pltpu.CompilerParams(vmem_limit_bytes=mib * 2**20, **more)


def one_hot(mask):
    return jnp.where(mask, 1.0, 0.0).astype(bf16)


def plan_slots(owner_ref, row_ref, slot_count, devices, mates):
    owner = jnp.concatenate([owner_ref[0], owner_ref[1]], axis=1)
    row = jnp.concatenate([row_ref[0:1, :], row_ref[1:2, :]], axis=1)
    requests = owner.shape[1]
    bits = int(math.log2(mates))
    place = (owner & (mates - 1)) * (devices // mates) + lax.shift_right_logical(owner, bits)
    named = iota((devices, requests), 0) == place
    named_hot = one_hot(named)
    earlier = one_hot(iota((requests, requests), 0) < iota((requests, requests), 1))
    before = dot(named_hot, earlier, 1, 0)
    rank = jnp.sum(jnp.where(named, before, 0.0), axis=0, keepdims=True).astype(i32)
    high = lax.shift_right_logical(row, 6)
    low = row - high * 64
    lane = iota((lanes, requests), 0)
    parts = jnp.where(lane == rank, high.astype(f32), 0.0)
    parts = parts + jnp.where(lane == rank + slot_count, low.astype(f32), 0.0)
    return owner * slot_count + rank, dot(named_hot, parts.astype(bf16), 1, 1)


def asked_column(asked, slot_count):
    devices = asked.shape[0]
    rows = devices * slot_count
    group = lax.shift_right_logical(iota((rows, devices), 0), int(math.log2(slot_count)))
    pick = one_hot(group == iota((rows, devices), 1))
    spread = dot(pick, asked.astype(bf16), 1, 0)
    slot = iota((rows, lanes), 0) & (slot_count - 1)
    lane = iota((rows, lanes), 1)
    row = jnp.where(lane == slot, spread * 64.0, jnp.where(lane == slot + slot_count, spread, 0.0))
    return jnp.sum(row, axis=1, keepdims=True).astype(i32)


def column_of(row):
    size = row.shape[1]
    here = iota((size, size), 0) == iota((size, size), 1)
    return jnp.sum(jnp.where(here, row.astype(f32), 0.0), axis=1, keepdims=True).astype(i32)


def softplus(x):
    return jnp.maximum(x, 0.0) + jnp.log1p(jnp.exp(-jnp.abs(x)))


def fetch_kernel(
    slot_count, table_size, group_size,
    owner_hbm, row_hbm, neg_hbm, ids_hbm, type_hbm, table_hbm, center_hbm, offset_hbm,
    asked_ref, slot_ref, back_ref, block_ref, shift_ref, size_ref,
    owner_ref, row_ref, neg_ref, ids_ref, type_ref, table, center_tab, offset_tab, center_sum, offset_rows, wanted, passed, ordered, served, column,
    load_sems, first_send, first_recv, second_send, second_recv, row_send, row_recv,
    pool_send, pool_recv,
):
    hops, queries = ids_ref.shape
    width, rels = center_tab.shape
    entities = table.shape[1]
    devices = table_size * group_size
    mates = 2 * group_size
    teams = devices // mates
    row_me, col_me = lax.axis_index("table"), lax.axis_index("blk")
    me = row_me * group_size + col_me
    mate, team = lax.rem(me, mates), lax.div(me, mates)

    def target(index):
        return (lax.div(index, group_size), lax.rem(index, group_size))

    loads = [
        pltpu.make_async_copy(source, place, load_sems.at[i])
        for i, (source, place) in enumerate(
            [
                (table_hbm, table), (center_hbm, center_tab), (offset_hbm, offset_tab),
                (owner_hbm, owner_ref), (row_hbm, row_ref), (neg_hbm, neg_ref),
                (ids_hbm, ids_ref), (type_hbm, type_ref),
            ]
        )
    ]
    for load in loads[3:] + loads[:3]:
        load.start()

    barrier = pltpu.get_barrier_semaphore()

    def greet(i, _):
        pl.semaphore_signal(
            barrier, inc=1, device_id=target(lax.rem(me + i, devices)), device_id_type=MESH
        )
        return 0

    lax.fori_loop(1, devices, greet, 0)

    for load in loads[3:]:
        load.wait()
    slot, asked = plan_slots(owner_ref, row_ref, slot_count, devices, mates)
    slot_ref[...] = slot
    wanted[...] = asked.reshape(mates, teams, lanes)
    center_sum[...] = jnp.zeros_like(center_sum)
    offset_rows[...] = jnp.zeros_like(offset_rows)

    pl.semaphore_wait(barrier, devices - 1)

    def first_hop(i, _):
        other = lax.rem(mate + i, mates)
        pltpu.make_async_remote_copy(
            src_ref=wanted.at[other], dst_ref=passed.at[mate],
            send_sem=first_send, recv_sem=first_recv,
            device_id=target(team * mates + other), device_id_type=MESH,
        ).start()
        return 0

    lax.fori_loop(1, mates, first_hop, 0)

    loads[0].wait()

    def rows_at(rows):
        total = None
        for start in range(0, entities, 1024):
            hot = one_hot(iota((rows.shape[0], 1024), 1) + start == rows)
            part = dot(hot, table[:, start : start + 1024], 1, 1)
            total = part if total is None else total + part
        return total.astype(bf16)

    block_ref[0] = rows_at(column_of(neg_ref[...]))
    pool_copies = []
    for step in range(1, group_size):
        copy = pltpu.make_async_remote_copy(
            src_ref=block_ref.at[0], dst_ref=block_ref.at[step],
            send_sem=pool_send.at[step], recv_sem=pool_recv.at[step],
            device_id=(row_me, lax.rem(col_me + step, group_size)), device_id_type=MESH,
        )
        copy.start()
        pool_copies.append(copy)

    def await_all(ref, count, sem):
        part = ref.at[pl.ds(0, count)]
        pltpu.make_async_copy(part, part, sem).wait()

    def relations(base, size):
        columns = pl.ds(base, size)
        count = jnp.zeros((size, queries), f32)
        hots = []
        for hop in range(hops):
            hot = jnp.where(iota((size, queries), 0) + base == ids_ref[hop : hop + 1, :], 1.0, 0.0)
            hots.append(hot.astype(bf16))
            count = count + jnp.where(type_ref[...] >= hop, hot, 0.0)
        center_sum[...] += dot(center_tab[:, columns], count.astype(bf16), 1, 0)
        for hop in range(hops):
            here = pl.ds(hop * queries, queries)
            offset_rows[:, here] += dot(offset_tab[:, columns], hots[hop], 1, 0)

    step = 1024
    whole_steps = rels // step
    cuts = (0, 2, 4, whole_steps)

    def relations_part(i):
        def body(k, _):
            relations(pl.multiple_of(k * step, step), step)
            return 0

        lax.fori_loop(cuts[i], cuts[i + 1], body, 0)

    passed[mate] = wanted[mate]
    await_all(wanted, mates - 1, first_send)
    await_all(passed, mates - 1, first_recv)
    source, target_row = iota((devices, devices), 1), iota((devices, devices), 0)
    mate_bits, team_bits = int(math.log2(mates)), int(math.log2(teams))
    order = one_hot(
        (target_row & (mates - 1)) * teams + lax.shift_right_logical(target_row, mate_bits) == source
    )
    ordered[...] = dot(order, passed[...].reshape(devices, lanes).astype(bf16), 1, 0).reshape(
        teams, mates, lanes
    )

    def second_hop(i, _):
        other = lax.rem(team + i, teams)
        pltpu.make_async_remote_copy(
            src_ref=ordered.at[other], dst_ref=asked_ref.at[team],
            send_sem=second_send, recv_sem=second_recv,
            device_id=target(other * mates + mate), device_id_type=MESH,
        ).start()
        return 0

    lax.fori_loop(1, teams, second_hop, 0)
    loads[1].wait()
    loads[2].wait()
    relations_part(0)
    asked_ref[team] = ordered[team]
    await_all(ordered, teams - 1, second_send)
    await_all(asked_ref, teams - 1, second_recv)

    column[...] = asked_column(asked_ref[...].reshape(devices, lanes), slot_count)
    quarter = devices // 4
    mine, inside = lax.div(me, quarter), lax.rem(me, quarter)
    for turn in (1, 2, 3, 0):
        part = lax.rem(mine + turn, 4)
        size = quarter * slot_count
        rows = rows_at(column[pl.ds(pl.multiple_of(part * size, size), size), :])
        served[pl.ds(part * quarter, quarter)] = rows.reshape(quarter, slot_count, width)

        def send_rows(i, _):
            other = part * quarter + lax.rem(inside + i, quarter)
            pltpu.make_async_remote_copy(
                src_ref=served.at[other], dst_ref=back_ref.at[me],
                send_sem=row_send, recv_sem=row_recv,
                device_id=target(other), device_id_type=MESH,
            ).start()
            return 0

        lax.fori_loop(1 if turn == 0 else 0, quarter, send_rows, 0)

    back_ref[me] = served[me]
    relations_part(1)
    relations_part(2)
    if rels % step:
        relations(whole_steps * step, rels % step)
    shift_ref[...] = center_sum[...]
    total = jnp.zeros((width, queries), f32)
    for hop in range(hops):
        value = softplus(offset_rows[:, hop * queries : (hop + 1) * queries])
        total = total + jnp.where(type_ref[...] >= hop, value, 0.0)
    size_ref[...] = total
    for copy in pool_copies:
        copy.wait()
    await_all(served, devices - 1, row_send)
    await_all(back_ref, devices - 1, row_recv)


def slope_terms(gap, size):
    square = gap * gap + scaled_eps
    inverse = lax.rsqrt(square)
    spread = square * inverse
    above = 1.0 + jnp.exp2(spread - size)
    slope = (1.0 / slope_weight - pl.reciprocal(above, approx=True)) * (gap * inverse)
    return spread, above, slope


def grads_kernel(table_size, group_size, slot_ref, back_ref, block_ref, shift_ref, size_ref,
                 returned_ref, pool_ref, entity, picks, spread_out, center, size, grads, slopes, dists, weights, pool_grad, codes,
                 coded, pool_rows, row_send, row_recv, pool_send, pool_recv):
    width, queries = shift_ref.shape
    rows = back_ref.shape[0] * back_ref.shape[1]
    negatives = block_ref.shape[0] * block_ref.shape[1]
    tiles = width // 8
    devices = table_size * group_size
    row_me, col_me = lax.axis_index("table"), lax.axis_index("blk")
    me = row_me * group_size + col_me

    def target(index):
        return (lax.div(index, group_size), lax.rem(index, group_size))

    hot = one_hot(iota((rows, 2 * queries), 0) == slot_ref[...])
    picked = dot(back_ref[...].reshape(rows, width), hot, 0, 0)
    center[...] = (picked[:, 0:queries] + shift_ref[...]) * log2e
    size[...] = size_ref[...] * log2e
    grads[:, queries:] = picked[:, queries:] * log2e
    eye = one_hot(iota((negatives, negatives), 0) == iota((negatives, negatives), 1))
    columns = dot(block_ref[...].reshape(negatives, width), eye, 0, 0) * log2e
    high = columns.astype(bf16)
    entity[:, 0:negatives] = high
    entity[:, negatives:] = (columns - high.astype(f32)).astype(bf16)
    pool_grad[...] = jnp.zeros_like(pool_grad)

    spread, above, slope = slope_terms(grads[:, queries:] - center[...], size[...])
    total = jnp.sum(spread + log_weight * jnp.log2(above), axis=0, keepdims=True) * dist_unit
    weight = (loss_scale * dist_scale * slope_weight) / (1.0 + jnp.exp(margin_gamma - total))
    slope = slope * weight
    grads[:, 0:queries] = -slope
    grads[:, queries:] = slope

    halves = [pl.ds(half * lanes, lanes) for half in range(queries // lanes)]
    lane = iota((8, lanes), 1)
    group = 4
    reach = 50

    def pick(j):
        source = iota((2 * negatives, near * lanes), 0) & (negatives - 1)
        target = lax.shift_right_logical(iota(source.shape, 1), 7)
        return one_hot(source == j * near + target)

    spread_out[0] = dot(entity[...], pick(0), 1, 0)

    def chunk(j, _):
        here = j * near
        now = lax.rem(j, 2)
        for first in range(0, near, group):
            def forward(base, count, sums):
                sums = list(sums)
                for k in range(group):
                    at = first + k
                    for half, ql in enumerate(halves):
                        total = sums[half * group + k]
                        product = None
                        for tile in range(count):
                            d = pl.ds(base + tile * 8, 8)
                            column = spread_out[now, d, at * lanes : (at + 1) * lanes]
                            spread, above, slope = slope_terms(column - center[d, ql], size[d, ql])
                            slopes[at, d, ql] = slope
                            product = above if product is None else product * above
                            total = total + spread
                            if tile % 4 == 3 or tile == count - 1:
                                total = total + log_weight * jnp.log2(product)
                                product = None
                        sums[half * group + k] = total
                return tuple(sums)

            sums = tuple(jnp.zeros((8, lanes), f32) for _ in range(group * len(halves)))
            for start in range(0, tiles, reach):
                sums = forward(start * 8, min(reach, tiles - start), sums)
            for half, ql in enumerate(halves):
                for k in range(group):
                    dists[first + k : first + k + 1, ql] = jnp.sum(
                        sums[half * group + k], axis=0, keepdims=True
                    )
        scale = -loss_scale * dist_scale * slope_weight / negatives
        weights[...] = scale / (1.0 + jnp.exp(dists[...] * dist_unit - margin_gamma))
        weight_rows = [
            [jnp.broadcast_to(weights[k : k + 1, ql], (8, lanes)) for ql in halves]
            for k in range(near)
        ]

        picks[...] = pick(j + 1)

        spread_out[1 - now] = dot(entity[...], picks[...], 1, 0)
        for tile in range(tiles):
            d = pl.ds(tile * 8, 8)
            to_center = [grads[d, ql] for ql in halves]
            to_pool = pool_grad[d, :]
            for k in range(near):
                row = None
                for half, ql in enumerate(halves):
                    term = slopes[k, d, ql] * weight_rows[k][half]
                    to_center[half] = to_center[half] - term
                    row = term if row is None else row + term
                row = jnp.sum(row, axis=1, keepdims=True)
                to_pool = jnp.where(lane == here + k, row, to_pool)
            for half, ql in enumerate(halves):
                grads[d, ql] = to_center[half]
            pool_grad[d, :] = to_pool
        return 0

    lax.fori_loop(0, negatives // near, chunk, 0)

    value = grads[...]
    most = jnp.max(jnp.abs(value), axis=0, keepdims=True)
    power = 14.0 - jnp.floor(jnp.log2(jnp.maximum(most, 1e-30)))
    level = jnp.minimum(jnp.maximum(jnp.round(value * jnp.exp2(power)), -32767.0), 32767.0)
    high = jnp.floor(level * (1.0 / 256.0) + 0.5)
    low = level - high * 256.0
    codes[...] = jnp.zeros_like(codes)
    codes[0:width, 0 : 2 * queries] = high.astype(bf16)
    codes[0:width, 2 * queries :] = low.astype(bf16)
    codes[width : width + 16, 2 * queries :] = jnp.broadcast_to(power, (16, 2 * queries)).astype(bf16)
    for step in range(group_size):
        pool_rows[step] = jnp.transpose(
            pool_grad[...]
        )[step * negatives // group_size : (step + 1) * negatives // group_size, 0:width]
    copies = []
    for step in range(1, group_size):
        copy = pltpu.make_async_remote_copy(
            src_ref=pool_rows.at[step], dst_ref=pool_ref.at[step],
            send_sem=pool_send.at[step], recv_sem=pool_recv.at[step],
            device_id=(row_me, lax.rem(col_me + group_size - step, group_size)),
            device_id_type=MESH,
        )
        copy.start()
        copies.append(copy)

    slot_count = rows // devices
    quarter = devices // 4
    mine, inside = lax.div(me, quarter), lax.rem(me, quarter)
    for turn in (1, 2, 3, 0):
        part = lax.rem(mine + turn, 4)
        size = quarter * slot_count
        chosen = one_hot(iota((size, 2 * queries), 0) + part * size == slot_ref[...])
        level = dot(chosen, codes[:, 0 : 2 * queries], 1, 1) * 256.0
        level = level + dot(chosen, codes[:, 2 * queries :], 1, 1)
        level = level.astype(i32).astype(jnp.int16)
        coded[pl.ds(part * quarter, quarter)] = level.reshape(quarter, slot_count, codes.shape[0])

        def send_rows(i, _):
            other = part * quarter + lax.rem(inside + i, quarter)
            pltpu.make_async_remote_copy(
                src_ref=coded.at[other], dst_ref=returned_ref.at[me],
                send_sem=row_send, recv_sem=row_recv,
                device_id=target(other), device_id_type=MESH,
            ).start()
            return 0

        lax.fori_loop(1 if turn == 0 else 0, quarter, send_rows, 0)

    returned_ref[me] = coded[me]
    pool_ref[0] = pool_rows[0]
    for copy in copies:
        copy.wait()
    sent, got = coded.at[pl.ds(0, devices - 1)], returned_ref.at[pl.ds(0, devices - 1)]
    pltpu.make_async_copy(sent, sent, row_send).wait()
    pltpu.make_async_copy(got, got, row_recv).wait()


def step_kernel(slot_count, table_size, group_size, *refs):
    sources, (asked_ref, returned_ref, pool_ref), scratch = refs[0:8], refs[8:11], refs[11:]
    boxes, fetching, grading = scratch[0:5], scratch[5:29], scratch[29:]
    fetch_kernel(slot_count, table_size, group_size, *sources, asked_ref, *boxes, *fetching)
    grads_kernel(table_size, group_size, *boxes, returned_ref, pool_ref, *grading)


def step(owner, row, neg_row, rel_ids, query_type, table, rel_center, rel_offset, slot_count,
         table_size, group_size):
    hops, queries = rel_ids.shape
    width, rels = rel_center.shape
    entities = table.shape[1]
    devices = table_size * group_size
    mates = 2 * group_size
    teams = devices // mates
    pool = neg_row.shape[1]
    negatives = group_size * pool
    padded = -(-width // lanes) * lanes
    dma = pltpu.SemaphoreType.DMA
    boxes = [
        pltpu.VMEM((1, 2 * queries), i32),
        pltpu.VMEM((devices, slot_count, width), bf16),
        pltpu.VMEM((group_size, pool, width), bf16),
        pltpu.VMEM((width, queries), f32),
        pltpu.VMEM((width, queries), f32),
    ]
    fetching = [
        pltpu.VMEM(owner.shape, i32),
        pltpu.VMEM(row.shape, i32),
        pltpu.VMEM(neg_row.shape, i32),
        pltpu.VMEM(rel_ids.shape, i32),
        pltpu.VMEM(query_type.shape, i32),
        pltpu.VMEM((width, entities), bf16),
        pltpu.VMEM((width, rels), bf16),
        pltpu.VMEM((width, rels), bf16),
        pltpu.VMEM((width, queries), f32),
        pltpu.VMEM((width, hops * queries), f32),
        pltpu.VMEM((mates, teams, lanes), f32),
        pltpu.VMEM((mates, teams, lanes), f32),
        pltpu.VMEM((teams, mates, lanes), f32),
        pltpu.VMEM((devices, slot_count, width), bf16),
        pltpu.VMEM((devices * slot_count, 1), i32),
        dma((8,)), dma, dma, dma, dma, dma, dma, dma((group_size,)), dma((group_size,)),
    ]
    grading = [
        pltpu.VMEM((width, 2 * negatives), bf16),
        pltpu.VMEM((2 * negatives, near * lanes), bf16),
        pltpu.VMEM((2, width, near * lanes), f32),
        pltpu.VMEM((width, queries), f32),
        pltpu.VMEM((width, queries), f32),
        pltpu.VMEM((width, 2 * queries), f32),
        pltpu.VMEM((near, width, queries), f32),
        pltpu.VMEM((near, queries), f32),
        pltpu.VMEM((near, queries), f32),
        pltpu.VMEM((padded, negatives), f32),
        pltpu.VMEM((padded, 4 * queries), bf16),
        pltpu.VMEM((devices, slot_count, padded), jnp.int16),
        pltpu.VMEM((group_size, pool, width), f32),
        dma, dma, dma((group_size,)), dma((group_size,)),
    ]
    scratch = boxes + fetching + grading
    return pl.pallas_call(
        functools.partial(step_kernel, slot_count, table_size, group_size),
        out_shape=(
            jax.ShapeDtypeStruct((teams, mates, lanes), f32),
            jax.ShapeDtypeStruct((devices, slot_count, padded), jnp.int16),
            jax.ShapeDtypeStruct((group_size, pool, width), f32),
        ),
        in_specs=[pl.BlockSpec(memory_space=pltpu.HBM)] * 8,
        out_specs=(whole(),) * 3,
        scratch_shapes=scratch,
        compiler_params=params(56, collective_id=0, has_side_effects=True),
        name="step",
    )(owner, row, neg_row, rel_ids, query_type, table, rel_center, rel_offset)


def scatter_kernel(slot_count, asked_ref, neg_ref, back_ref, pool_ref, out_ref, column, rows_of, both):
    step = pl.program_id(0)
    width, part = out_ref.shape
    rows, padded = back_ref.shape
    group_size, pool = pool_ref.shape[0:2]

    @pl.when(step == 0)
    def _():
        column[0:rows, :] = asked_column(asked_ref[...], slot_count)
        column[rows : rows + pool, :] = column_of(neg_ref[...])
        column[rows + pool :, :] = jnp.full((lanes - pool, 1), -1, i32)
        level = back_ref[...].astype(i32).astype(f32)
        rows_of[0:rows, :] = level * jnp.exp2(-level[:, width : width + 1])
        rows_of[rows:, :] = jnp.zeros((lanes, padded), f32)
        rows_of[rows : rows + pool, 0:width] = sum(pool_ref[i] for i in range(group_size))
        value = jnp.transpose(rows_of[...])[0:width, :]
        high = value.astype(bf16)
        both[0:width, :] = high
        both[width:, :] = (value - high.astype(f32)).astype(bf16)

    hot = one_hot(iota((rows + lanes, part), 1) == column[...] - step * part)
    result = dot(both[...], hot, 1, 0)
    out_ref[...] = result[0:width, :] + result[width:, :]


def scatter(asked, neg_rows, back, pools, slot_count, entities):
    rows, padded = back.shape
    width = pools.shape[2]
    part = 1024
    fixed = lambda i: (0, 0)
    return pl.pallas_call(
        functools.partial(scatter_kernel, slot_count),
        out_shape=jax.ShapeDtypeStruct((width, entities), f32),
        grid=(entities // part,),
        in_specs=[
            pl.BlockSpec(asked.shape, fixed),
            pl.BlockSpec(neg_rows.shape, fixed),
            pl.BlockSpec((rows, padded), fixed),
            pl.BlockSpec(pools.shape, lambda i: (0, 0, 0)),
        ],
        out_specs=pl.BlockSpec((width, part), lambda i: (0, i)),
        scratch_shapes=[
            pltpu.VMEM((rows + lanes, 1), i32),
            pltpu.VMEM((rows + lanes, padded), f32),
            pltpu.VMEM((2 * width, rows + lanes), bf16),
        ],
        compiler_params=params(48),
        name="scatter",
    )(asked, neg_rows, back, pools)


def local(
    entity_table, rel_center, rel_offset, entity_owner, entity_row, rel_ids, query_type, neg_rows
):
    entities, width = entity_table.shape
    table_size = lax.axis_size("table")
    group_size = lax.axis_size("blk")
    devices = table_size * group_size
    queries = rel_ids.shape[0]
    slot_count = 4 * queries // devices
    pool = neg_rows.shape[0]
    table = entity_table.T
    neg_row = neg_rows.reshape(1, pool)
    asked, returned, pool_grads = step(
        entity_owner.transpose(1, 2, 0), entity_row.T, neg_row, rel_ids.T,
        query_type.reshape(1, queries), table, rel_center.T, rel_offset.T, slot_count,
        table_size, group_size,
    )
    asked = asked.reshape(devices, lanes)
    returned = returned.reshape(devices * slot_count, -1)
    return scatter(asked, neg_row, returned, pool_grads, slot_count, entities).T


def solution(mesh):
    placed = (
        P(("table", "blk"), None),
        P(),
        P(),
        P(("table", "blk"), None, None),
        P(("table", "blk"), None),
        P(("table", "blk"), None),
        P(("table", "blk")),
        P(("table", "blk")),
    )
    return jax.shard_map(
        local, mesh=mesh, in_specs=placed, out_specs=P(("table", "blk"), None), check_vma=False
    )
```

```python
import functools
import math
import jax
import jax.numpy as jnp
from jax import lax
from jax.experimental import pallas as pl
from jax.experimental.pallas import tpu as pltpu
from jax.sharding import PartitionSpec as P

margin_gamma = 7.0
dist_scale = 0.02
inside_weight = 0.2
smooth_eps = 0.01
loss_scale = 64.0

f32 = jnp.float32
bf16 = jnp.bfloat16
i32 = jnp.int32
log2e = math.log2(math.e)
scaled_eps = smooth_eps * log2e * log2e
dist_unit = dist_scale * math.log(2.0) * inside_weight
log_weight = (1.0 - inside_weight) / inside_weight
slope_weight = 1.0 - inside_weight
lanes = 128
MESH = pl.DeviceIdType.MESH
near = 8


def iota(shape, axis):
    return lax.broadcasted_iota(i32, shape, axis)


def dot(a, b, ca, cb):
    return lax.dot_general(a, b, (((ca,), (cb,)), ((), ())), preferred_element_type=f32)


def whole():
    return pl.BlockSpec(memory_space=pltpu.VMEM)


def params(mib, **more):
    return pltpu.CompilerParams(vmem_limit_bytes=mib * 2**20, **more)


def one_hot(mask):
    return jnp.where(mask, 1.0, 0.0).astype(bf16)


def plan_slots(owner_ref, row_ref, slot_count, devices, mates):
    owner = jnp.concatenate([owner_ref[0], owner_ref[1]], axis=1)
    row = jnp.concatenate([row_ref[0:1, :], row_ref[1:2, :]], axis=1)
    requests = owner.shape[1]
    bits = int(math.log2(mates))
    place = (owner & (mates - 1)) * (devices // mates) + lax.shift_right_logical(owner, bits)
    named = iota((devices, requests), 0) == place
    named_hot = one_hot(named)
    earlier = one_hot(iota((requests, requests), 0) < iota((requests, requests), 1))
    before = dot(named_hot, earlier, 1, 0)
    rank = jnp.sum(jnp.where(named, before, 0.0), axis=0, keepdims=True).astype(i32)
    high = lax.shift_right_logical(row, 6)
    low = row - high * 64
    lane = iota((lanes, requests), 0)
    parts = jnp.where(lane == rank, high.astype(f32), 0.0)
    parts = parts + jnp.where(lane == rank + slot_count, low.astype(f32), 0.0)
    return owner * slot_count + rank, dot(named_hot, parts.astype(bf16), 1, 1)


def partner(position, row_me, col_me):
    def part(value, size):
        return value - lax.div(value, jnp.full_like(value, size)) * size

    def over(value, size):
        return lax.div(value, jnp.full_like(value, size))

    core, depth, rest = part(position, 2), part(over(position, 2), 4), over(position, 8)
    line, plane = part(rest, 4), over(rest, 4)
    y = part(over(row_me, 2) + line + depth, 4)
    x = part(over(row_me, 8) + plane + depth + 2 * line, 4)
    core = part(row_me + core, 2)
    return (x * 4 + y) * 2 + core, part(col_me + depth, 4)


def partner_index(position, row_me, col_me, group_size):
    row, col = partner(position, row_me, col_me)
    return row * group_size + col


def asked_column(asked, slot_count, order=None):
    devices = asked.shape[0]
    rows = devices * slot_count
    group = lax.shift_right_logical(iota((rows, 1), 0), int(math.log2(slot_count)))
    if order is not None:
        group = order(group)
    pick = one_hot(group == iota((rows, devices), 1))
    spread = dot(pick, asked.astype(bf16), 1, 0)
    slot = iota((rows, lanes), 0) & (slot_count - 1)
    lane = iota((rows, lanes), 1)
    row = jnp.where(lane == slot, spread * 64.0, jnp.where(lane == slot + slot_count, spread, 0.0))
    return jnp.sum(row, axis=1, keepdims=True).astype(i32)


def column_of(row):
    size = row.shape[1]
    here = iota((size, size), 0) == iota((size, size), 1)
    return jnp.sum(jnp.where(here, row.astype(f32), 0.0), axis=1, keepdims=True).astype(i32)


def softplus(x):
    return jnp.maximum(x, 0.0) + jnp.log1p(jnp.exp(-jnp.abs(x)))


def fetch_kernel(
    slot_count, table_size, group_size,
    owner_hbm, row_hbm, neg_hbm, ids_hbm, type_hbm, table_hbm, center_hbm, offset_hbm,
    asked_ref, slot_ref, back_ref, block_ref, shift_ref, size_ref,
    owner_ref, row_ref, neg_ref, ids_ref, type_ref, table, center_tab, offset_tab, center_sum, offset_rows, wanted, passed, ordered, served, column,
    load_sems, first_send, first_recv, second_send, second_recv, row_send, row_recv,
    pool_send, pool_recv,
):
    hops, queries = ids_ref.shape
    width, rels = center_tab.shape
    entities = table.shape[1]
    devices = table_size * group_size
    mates = 2 * group_size
    teams = devices // mates
    row_me, col_me = lax.axis_index("table"), lax.axis_index("blk")
    me = row_me * group_size + col_me
    mate, team = lax.rem(me, mates), lax.div(me, mates)

    def target(index):
        return (lax.div(index, group_size), lax.rem(index, group_size))

    loads = [
        pltpu.make_async_copy(source, place, load_sems.at[i])
        for i, (source, place) in enumerate(
            [
                (table_hbm, table), (center_hbm, center_tab), (offset_hbm, offset_tab),
                (owner_hbm, owner_ref), (row_hbm, row_ref), (neg_hbm, neg_ref),
                (ids_hbm, ids_ref), (type_hbm, type_ref),
            ]
        )
    ]
    for load in loads[3:] + loads[:3]:
        load.start()

    barrier = pltpu.get_barrier_semaphore()

    def greet(i, _):
        pl.semaphore_signal(
            barrier, inc=1, device_id=target(lax.rem(me + i, devices)), device_id_type=MESH
        )
        return 0

    lax.fori_loop(1, devices, greet, 0)

    for load in loads[3:]:
        load.wait()
    slot, asked = plan_slots(owner_ref, row_ref, slot_count, devices, mates)
    slot_ref[...] = slot
    wanted[...] = asked.reshape(mates, teams, lanes)
    center_sum[...] = jnp.zeros_like(center_sum)
    offset_rows[...] = jnp.zeros_like(offset_rows)

    pl.semaphore_wait(barrier, devices - 1)

    def first_hop(i, _):
        other = lax.rem(mate + i, mates)
        pltpu.make_async_remote_copy(
            src_ref=wanted.at[other], dst_ref=passed.at[mate],
            send_sem=first_send, recv_sem=first_recv,
            device_id=target(team * mates + other), device_id_type=MESH,
        ).start()
        return 0

    lax.fori_loop(1, mates, first_hop, 0)

    loads[0].wait()

    def rows_at(rows):
        total = None
        for start in range(0, entities, 1024):
            hot = one_hot(iota((rows.shape[0], 1024), 1) + start == rows)
            part = dot(hot, table[:, start : start + 1024], 1, 1)
            total = part if total is None else total + part
        return total.astype(bf16)

    block_ref[0] = rows_at(column_of(neg_ref[...]))
    pool_copies = []
    for step in range(1, group_size):
        copy = pltpu.make_async_remote_copy(
            src_ref=block_ref.at[0], dst_ref=block_ref.at[step],
            send_sem=pool_send.at[step], recv_sem=pool_recv.at[step],
            device_id=(row_me, lax.rem(col_me + step, group_size)), device_id_type=MESH,
        )
        copy.start()
        pool_copies.append(copy)

    def await_all(ref, count, sem):
        part = ref.at[pl.ds(0, count)]
        pltpu.make_async_copy(part, part, sem).wait()

    def relations(base, size):
        columns = pl.ds(base, size)
        count = jnp.zeros((size, queries), f32)
        hots = []
        for hop in range(hops):
            hot = jnp.where(iota((size, queries), 0) + base == ids_ref[hop : hop + 1, :], 1.0, 0.0)
            hots.append(hot.astype(bf16))
            count = count + jnp.where(type_ref[...] >= hop, hot, 0.0)
        center_sum[...] += dot(center_tab[:, columns], count.astype(bf16), 1, 0)
        for hop in range(hops):
            here = pl.ds(hop * queries, queries)
            offset_rows[:, here] += dot(offset_tab[:, columns], hots[hop], 1, 0)

    step = 1024
    whole_steps = rels // step
    cuts = (0, 2, 4, whole_steps)

    def relations_part(i):
        def body(k, _):
            relations(pl.multiple_of(k * step, step), step)
            return 0

        lax.fori_loop(cuts[i], cuts[i + 1], body, 0)

    passed[mate] = wanted[mate]
    await_all(wanted, mates - 1, first_send)
    await_all(passed, mates - 1, first_recv)
    source, target_row = iota((devices, devices), 1), iota((devices, devices), 0)
    mate_bits, team_bits = int(math.log2(mates)), int(math.log2(teams))
    order = one_hot(
        (target_row & (mates - 1)) * teams + lax.shift_right_logical(target_row, mate_bits) == source
    )
    ordered[...] = dot(order, passed[...].reshape(devices, lanes).astype(bf16), 1, 0).reshape(
        teams, mates, lanes
    )

    def second_hop(i, _):
        other = lax.rem(team + i, teams)
        pltpu.make_async_remote_copy(
            src_ref=ordered.at[other], dst_ref=asked_ref.at[team],
            send_sem=second_send, recv_sem=second_recv,
            device_id=target(other * mates + mate), device_id_type=MESH,
        ).start()
        return 0

    lax.fori_loop(1, teams, second_hop, 0)
    loads[1].wait()
    loads[2].wait()
    relations_part(0)
    asked_ref[team] = ordered[team]
    await_all(ordered, teams - 1, second_send)
    await_all(asked_ref, teams - 1, second_recv)

    column[...] = asked_column(
        asked_ref[...].reshape(devices, lanes), slot_count,
        lambda group: partner_index(group, row_me, col_me, group_size),
    )
    quarter = devices // 4

    def send_rows(i, _):
        pltpu.make_async_remote_copy(
            src_ref=served.at[i], dst_ref=back_ref.at[me],
            send_sem=row_send, recv_sem=row_recv,
            device_id=partner(i, row_me, col_me), device_id_type=MESH,
        ).start()
        return 0

    for part in (1, 2, 3, 0):
        size = quarter * slot_count
        rows = rows_at(column[part * size : (part + 1) * size, :])
        served[part * quarter : (part + 1) * quarter] = rows.reshape(quarter, slot_count, width)
        lax.fori_loop(max(1, part * quarter), (part + 1) * quarter, send_rows, 0)

    back_ref[me] = served[0]
    relations_part(1)
    relations_part(2)
    if rels % step:
        relations(whole_steps * step, rels % step)
    shift_ref[...] = center_sum[...]
    total = jnp.zeros((width, queries), f32)
    for hop in range(hops):
        value = softplus(offset_rows[:, hop * queries : (hop + 1) * queries])
        total = total + jnp.where(type_ref[...] >= hop, value, 0.0)
    size_ref[...] = total
    for copy in pool_copies:
        copy.wait()
    await_all(served, devices - 1, row_send)
    await_all(back_ref, devices - 1, row_recv)


def slope_terms(gap, size):
    square = gap * gap + scaled_eps
    inverse = lax.rsqrt(square)
    spread = square * inverse
    above = 1.0 + jnp.exp2(spread - size)
    slope = (1.0 / slope_weight - pl.reciprocal(above, approx=True)) * (gap * inverse)
    return spread, above, slope


def grads_kernel(table_size, group_size, slot_ref, back_ref, block_ref, shift_ref, size_ref,
                 returned_ref, pool_ref, entity, picks, spread_out, center, size, grads, slopes, dists, weights, pool_grad, codes,
                 coded, pool_rows, row_send, row_recv, pool_send, pool_recv):
    width, queries = shift_ref.shape
    rows = back_ref.shape[0] * back_ref.shape[1]
    negatives = block_ref.shape[0] * block_ref.shape[1]
    tiles = width // 8
    devices = table_size * group_size
    row_me, col_me = lax.axis_index("table"), lax.axis_index("blk")
    me = row_me * group_size + col_me

    def target(index):
        return (lax.div(index, group_size), lax.rem(index, group_size))

    hot = one_hot(iota((rows, 2 * queries), 0) == slot_ref[...])
    picked = dot(back_ref[...].reshape(rows, width), hot, 0, 0)
    center[...] = (picked[:, 0:queries] + shift_ref[...]) * log2e
    size[...] = size_ref[...] * log2e
    grads[:, queries:] = picked[:, queries:] * log2e
    eye = one_hot(iota((negatives, negatives), 0) == iota((negatives, negatives), 1))
    columns = dot(block_ref[...].reshape(negatives, width), eye, 0, 0) * log2e
    high = columns.astype(bf16)
    entity[:, 0:negatives] = high
    entity[:, negatives:] = (columns - high.astype(f32)).astype(bf16)
    pool_grad[...] = jnp.zeros_like(pool_grad)

    spread, above, slope = slope_terms(grads[:, queries:] - center[...], size[...])
    total = jnp.sum(spread + log_weight * jnp.log2(above), axis=0, keepdims=True) * dist_unit
    weight = (loss_scale * dist_scale * slope_weight) / (1.0 + jnp.exp(margin_gamma - total))
    slope = slope * weight
    grads[:, 0:queries] = -slope
    grads[:, queries:] = slope

    halves = [pl.ds(half * lanes, lanes) for half in range(queries // lanes)]
    lane = iota((8, lanes), 1)
    group = 4
    reach = 50

    def pick(j):
        source = iota((2 * negatives, near * lanes), 0) & (negatives - 1)
        target = lax.shift_right_logical(iota(source.shape, 1), 7)
        return one_hot(source == j * near + target)

    spread_out[0] = dot(entity[...], pick(0), 1, 0)

    def chunk(j, _):
        here = j * near
        now = lax.rem(j, 2)
        for first in range(0, near, group):
            def forward(base, count, sums):
                sums = list(sums)
                for k in range(group):
                    at = first + k
                    for half, ql in enumerate(halves):
                        total = sums[half * group + k]
                        product = None
                        for tile in range(count):
                            d = pl.ds(base + tile * 8, 8)
                            column = spread_out[now, d, at * lanes : (at + 1) * lanes]
                            spread, above, slope = slope_terms(column - center[d, ql], size[d, ql])
                            slopes[at, d, ql] = slope
                            product = above if product is None else product * above
                            total = total + spread
                            if tile % 4 == 3 or tile == count - 1:
                                total = total + log_weight * jnp.log2(product)
                                product = None
                        sums[half * group + k] = total
                return tuple(sums)

            sums = tuple(jnp.zeros((8, lanes), f32) for _ in range(group * len(halves)))
            for start in range(0, tiles, reach):
                sums = forward(start * 8, min(reach, tiles - start), sums)
            for half, ql in enumerate(halves):
                for k in range(group):
                    dists[first + k : first + k + 1, ql] = jnp.sum(
                        sums[half * group + k], axis=0, keepdims=True
                    )
        scale = -loss_scale * dist_scale * slope_weight / negatives
        weights[...] = scale / (1.0 + jnp.exp(dists[...] * dist_unit - margin_gamma))
        weight_rows = [
            [jnp.broadcast_to(weights[k : k + 1, ql], (8, lanes)) for ql in halves]
            for k in range(near)
        ]

        picks[...] = pick(j + 1)

        spread_out[1 - now] = dot(entity[...], picks[...], 1, 0)
        for tile in range(tiles):
            d = pl.ds(tile * 8, 8)
            to_center = [grads[d, ql] for ql in halves]
            to_pool = pool_grad[d, :]
            for k in range(near):
                row = None
                for half, ql in enumerate(halves):
                    term = slopes[k, d, ql] * weight_rows[k][half]
                    to_center[half] = to_center[half] - term
                    row = term if row is None else row + term
                row = jnp.sum(row, axis=1, keepdims=True)
                to_pool = jnp.where(lane == here + k, row, to_pool)
            for half, ql in enumerate(halves):
                grads[d, ql] = to_center[half]
            pool_grad[d, :] = to_pool
        return 0

    lax.fori_loop(0, negatives // near, chunk, 0)

    value = grads[...]
    most = jnp.max(jnp.abs(value), axis=0, keepdims=True)
    power = 14.0 - jnp.floor(jnp.log2(jnp.maximum(most, 1e-30)))
    level = jnp.minimum(jnp.maximum(jnp.round(value * jnp.exp2(power)), -32767.0), 32767.0)
    high = jnp.floor(level * (1.0 / 256.0) + 0.5)
    low = level - high * 256.0
    codes[...] = jnp.zeros_like(codes)
    codes[0:width, 0 : 2 * queries] = high.astype(bf16)
    codes[0:width, 2 * queries :] = low.astype(bf16)
    codes[width : width + 16, 2 * queries :] = jnp.broadcast_to(power, (16, 2 * queries)).astype(bf16)
    for step in range(group_size):
        pool_rows[step] = jnp.transpose(
            pool_grad[...]
        )[step * negatives // group_size : (step + 1) * negatives // group_size, 0:width]
    copies = []
    for step in range(1, group_size):
        copy = pltpu.make_async_remote_copy(
            src_ref=pool_rows.at[step], dst_ref=pool_ref.at[step],
            send_sem=pool_send.at[step], recv_sem=pool_recv.at[step],
            device_id=(row_me, lax.rem(col_me + group_size - step, group_size)),
            device_id_type=MESH,
        )
        copy.start()
        copies.append(copy)

    slot_count = rows // devices
    quarter = devices // 4

    def send_rows(i, _):
        pltpu.make_async_remote_copy(
            src_ref=coded.at[i], dst_ref=returned_ref.at[me],
            send_sem=row_send, recv_sem=row_recv,
            device_id=partner(i, row_me, col_me), device_id_type=MESH,
        ).start()
        return 0

    for part in range(4):
        size = quarter * slot_count
        place = iota((size, 1), 0) + part * size
        group = lax.shift_right_logical(place, int(math.log2(slot_count)))
        place = (place & (slot_count - 1)) + slot_count * partner_index(
            group, row_me, col_me, group_size
        )
        chosen = one_hot(place == slot_ref[...])
        level = dot(chosen, codes[:, 0 : 2 * queries], 1, 1) * 256.0
        level = level + dot(chosen, codes[:, 2 * queries :], 1, 1)
        level = level.astype(i32).astype(jnp.int16)
        coded[part * quarter : (part + 1) * quarter] = level.reshape(
            quarter, slot_count, codes.shape[0]
        )
        lax.fori_loop(max(1, part * quarter), (part + 1) * quarter, send_rows, 0)

    returned_ref[me] = coded[0]
    pool_ref[0] = pool_rows[0]
    for copy in copies:
        copy.wait()
    sent, got = coded.at[pl.ds(0, devices - 1)], returned_ref.at[pl.ds(0, devices - 1)]
    pltpu.make_async_copy(sent, sent, row_send).wait()
    pltpu.make_async_copy(got, got, row_recv).wait()


def step_kernel(slot_count, table_size, group_size, *refs):
    sources, (asked_ref, returned_ref, pool_ref), scratch = refs[0:8], refs[8:11], refs[11:]
    boxes, fetching, grading = scratch[0:5], scratch[5:29], scratch[29:]
    fetch_kernel(slot_count, table_size, group_size, *sources, asked_ref, *boxes, *fetching)
    grads_kernel(table_size, group_size, *boxes, returned_ref, pool_ref, *grading)


def step(owner, row, neg_row, rel_ids, query_type, table, rel_center, rel_offset, slot_count,
         table_size, group_size):
    hops, queries = rel_ids.shape
    width, rels = rel_center.shape
    entities = table.shape[1]
    devices = table_size * group_size
    mates = 2 * group_size
    teams = devices // mates
    pool = neg_row.shape[1]
    negatives = group_size * pool
    padded = -(-width // lanes) * lanes
    dma = pltpu.SemaphoreType.DMA
    boxes = [
        pltpu.VMEM((1, 2 * queries), i32),
        pltpu.VMEM((devices, slot_count, width), bf16),
        pltpu.VMEM((group_size, pool, width), bf16),
        pltpu.VMEM((width, queries), f32),
        pltpu.VMEM((width, queries), f32),
    ]
    fetching = [
        pltpu.VMEM(owner.shape, i32),
        pltpu.VMEM(row.shape, i32),
        pltpu.VMEM(neg_row.shape, i32),
        pltpu.VMEM(rel_ids.shape, i32),
        pltpu.VMEM(query_type.shape, i32),
        pltpu.VMEM((width, entities), bf16),
        pltpu.VMEM((width, rels), bf16),
        pltpu.VMEM((width, rels), bf16),
        pltpu.VMEM((width, queries), f32),
        pltpu.VMEM((width, hops * queries), f32),
        pltpu.VMEM((mates, teams, lanes), f32),
        pltpu.VMEM((mates, teams, lanes), f32),
        pltpu.VMEM((teams, mates, lanes), f32),
        pltpu.VMEM((devices, slot_count, width), bf16),
        pltpu.VMEM((devices * slot_count, 1), i32),
        dma((8,)), dma, dma, dma, dma, dma, dma, dma((group_size,)), dma((group_size,)),
    ]
    grading = [
        pltpu.VMEM((width, 2 * negatives), bf16),
        pltpu.VMEM((2 * negatives, near * lanes), bf16),
        pltpu.VMEM((2, width, near * lanes), f32),
        pltpu.VMEM((width, queries), f32),
        pltpu.VMEM((width, queries), f32),
        pltpu.VMEM((width, 2 * queries), f32),
        pltpu.VMEM((near, width, queries), f32),
        pltpu.VMEM((near, queries), f32),
        pltpu.VMEM((near, queries), f32),
        pltpu.VMEM((padded, negatives), f32),
        pltpu.VMEM((padded, 4 * queries), bf16),
        pltpu.VMEM((devices, slot_count, padded), jnp.int16),
        pltpu.VMEM((group_size, pool, width), f32),
        dma, dma, dma((group_size,)), dma((group_size,)),
    ]
    scratch = boxes + fetching + grading
    return pl.pallas_call(
        functools.partial(step_kernel, slot_count, table_size, group_size),
        out_shape=(
            jax.ShapeDtypeStruct((teams, mates, lanes), f32),
            jax.ShapeDtypeStruct((devices, slot_count, padded), jnp.int16),
            jax.ShapeDtypeStruct((group_size, pool, width), f32),
        ),
        in_specs=[pl.BlockSpec(memory_space=pltpu.HBM)] * 8,
        out_specs=(whole(),) * 3,
        scratch_shapes=scratch,
        compiler_params=params(56, collective_id=0, has_side_effects=True),
        name="step",
    )(owner, row, neg_row, rel_ids, query_type, table, rel_center, rel_offset)


def scatter_kernel(slot_count, asked_hbm, neg_hbm, back_hbm, pool_hbm, out_ref,
                   asked_ref, neg_ref, back_ref, pool_ref, column, rows_of, both, sems):
    step = pl.program_id(0)
    width, part = out_ref.shape
    rows, padded = back_ref.shape
    group_size, pool = pool_ref.shape[0:2]

    @pl.when(step == 0)
    def _():
        loads = [
            pltpu.make_async_copy(source, place, sems.at[i])
            for i, (source, place) in enumerate(
                [
                    (asked_hbm, asked_ref), (neg_hbm, neg_ref), (back_hbm, back_ref),
                    (pool_hbm, pool_ref),
                ]
            )
        ]
        for load in loads:
            load.start()
        loads[0].wait()
        column[0:rows, :] = asked_column(asked_ref[...], slot_count)
        loads[1].wait()
        column[rows : rows + pool, :] = column_of(neg_ref[...])
        column[rows + pool :, :] = jnp.full((lanes - pool, 1), -1, i32)
        loads[2].wait()
        level = back_ref[...].astype(i32).astype(f32)
        rows_of[0:rows, :] = level * jnp.exp2(-level[:, width : width + 1])
        rows_of[rows:, :] = jnp.zeros((lanes, padded), f32)
        loads[3].wait()
        rows_of[rows : rows + pool, 0:width] = sum(pool_ref[i] for i in range(group_size))
        value = jnp.transpose(rows_of[...])[0:width, :]
        high = value.astype(bf16)
        both[0:width, :] = high
        both[width:, :] = (value - high.astype(f32)).astype(bf16)

    hot = one_hot(iota((rows + lanes, part), 1) == column[...] - step * part)
    result = dot(both[...], hot, 1, 0)
    out_ref[...] = result[0:width, :] + result[width:, :]


def scatter(asked, neg_rows, back, pools, slot_count, entities):
    rows, padded = back.shape
    pool = neg_rows.shape[1]
    width = pools.shape[2]
    part = 1024
    return pl.pallas_call(
        functools.partial(scatter_kernel, slot_count),
        out_shape=jax.ShapeDtypeStruct((width, entities), f32),
        grid=(entities // part,),
        in_specs=[pl.BlockSpec(memory_space=pltpu.HBM)] * 4,
        out_specs=pl.BlockSpec((width, part), lambda i: (0, i)),
        scratch_shapes=[
            pltpu.VMEM(asked.shape, f32),
            pltpu.VMEM(neg_rows.shape, i32),
            pltpu.VMEM(back.shape, jnp.int16),
            pltpu.VMEM(pools.shape, f32),
            pltpu.VMEM((rows + lanes, 1), i32),
            pltpu.VMEM((rows + lanes, padded), f32),
            pltpu.VMEM((2 * width, rows + lanes), bf16),
            pltpu.SemaphoreType.DMA((4,)),
        ],
        compiler_params=params(56),
        name="scatter",
    )(asked, neg_rows, back, pools)


def local(
    entity_table, rel_center, rel_offset, entity_owner, entity_row, rel_ids, query_type, neg_rows
):
    entities, width = entity_table.shape
    table_size = lax.axis_size("table")
    group_size = lax.axis_size("blk")
    devices = table_size * group_size
    queries = rel_ids.shape[0]
    slot_count = 4 * queries // devices
    pool = neg_rows.shape[0]
    table = entity_table.T
    neg_row = neg_rows.reshape(1, pool)
    asked, returned, pool_grads = step(
        entity_owner.transpose(1, 2, 0), entity_row.T, neg_row, rel_ids.T,
        query_type.reshape(1, queries), table, rel_center.T, rel_offset.T, slot_count,
        table_size, group_size,
    )
    asked = asked.reshape(devices, lanes)
    returned = returned.reshape(devices * slot_count, -1)
    return scatter(asked, neg_row, returned, pool_grads, slot_count, entities).T


def solution(mesh):
    placed = (
        P(("table", "blk"), None),
        P(),
        P(),
        P(("table", "blk"), None, None),
        P(("table", "blk"), None),
        P(("table", "blk"), None),
        P(("table", "blk")),
        P(("table", "blk")),
    )
    return jax.shard_map(
        local, mesh=mesh, in_specs=placed, out_specs=P(("table", "blk"), None), check_vma=False
    )
```

```python
import functools
import math
import jax
import jax.numpy as jnp
from jax import lax
from jax.experimental import pallas as pl
from jax.experimental.pallas import tpu as pltpu
from jax.sharding import PartitionSpec as P

margin_gamma = 7.0
dist_scale = 0.02
inside_weight = 0.2
smooth_eps = 0.01
loss_scale = 64.0

f32 = jnp.float32
bf16 = jnp.bfloat16
i32 = jnp.int32
log2e = math.log2(math.e)
scaled_eps = smooth_eps * log2e * log2e
dist_unit = dist_scale * math.log(2.0) * inside_weight
log_weight = (1.0 - inside_weight) / inside_weight
slope_weight = 1.0 - inside_weight
lanes = 128
MESH = pl.DeviceIdType.MESH
near = 8


def iota(shape, axis):
    return lax.broadcasted_iota(i32, shape, axis)


def dot(a, b, ca, cb):
    return lax.dot_general(a, b, (((ca,), (cb,)), ((), ())), preferred_element_type=f32)


def whole():
    return pl.BlockSpec(memory_space=pltpu.VMEM)


def params(mib, **more):
    return pltpu.CompilerParams(vmem_limit_bytes=mib * 2**20, **more)


def one_hot(mask):
    return jnp.where(mask, 1.0, 0.0).astype(bf16)


def plan_slots(owner_ref, row_ref, slot_count, devices, mates):
    owner = jnp.concatenate([owner_ref[0], owner_ref[1]], axis=1)
    row = jnp.concatenate([row_ref[0:1, :], row_ref[1:2, :]], axis=1)
    requests = owner.shape[1]
    bits = int(math.log2(mates))
    place = (owner & (mates - 1)) * (devices // mates) + lax.shift_right_logical(owner, bits)
    named = iota((devices, requests), 0) == place
    named_hot = one_hot(named)
    earlier = one_hot(iota((requests, requests), 0) < iota((requests, requests), 1))
    before = dot(named_hot, earlier, 1, 0)
    rank = jnp.sum(jnp.where(named, before, 0.0), axis=0, keepdims=True).astype(i32)
    high = lax.shift_right_logical(row, 6)
    low = row - high * 64
    lane = iota((lanes, requests), 0)
    parts = jnp.where(lane == rank, high.astype(f32), 0.0)
    parts = parts + jnp.where(lane == rank + slot_count, low.astype(f32), 0.0)
    return owner * slot_count + rank, dot(named_hot, parts.astype(bf16), 1, 1)


def partner(position, row_me, col_me):
    def part(value, size):
        return value - lax.div(value, jnp.full_like(value, size)) * size

    def over(value, size):
        return lax.div(value, jnp.full_like(value, size))

    if isinstance(position, int):
        core, depth, line, plane = position % 2, position // 2 % 4, position // 8 % 4, position // 32
    else:
        core, depth, rest = part(position, 2), part(over(position, 2), 4), over(position, 8)
        line, plane = part(rest, 4), over(rest, 4)
    y = part(over(row_me, 2) + line + depth, 4)
    x = part(over(row_me, 8) + plane + depth + 2 * line, 4)
    core = part(row_me + core, 2)
    return (x * 4 + y) * 2 + core, part(col_me + depth, 4)


def partner_index(position, row_me, col_me, group_size):
    row, col = partner(position, row_me, col_me)
    return row * group_size + col


def asked_column(asked, slot_count, order=None):
    devices = asked.shape[0]
    rows = devices * slot_count
    group = lax.shift_right_logical(iota((rows, 1), 0), int(math.log2(slot_count)))
    if order is not None:
        group = order(group)
    pick = one_hot(group == iota((rows, devices), 1))
    spread = dot(pick, asked.astype(bf16), 1, 0)
    slot = iota((rows, lanes), 0) & (slot_count - 1)
    lane = iota((rows, lanes), 1)
    row = jnp.where(lane == slot, spread * 64.0, jnp.where(lane == slot + slot_count, spread, 0.0))
    return jnp.sum(row, axis=1, keepdims=True).astype(i32)


def column_of(row):
    size = row.shape[1]
    here = iota((size, size), 0) == iota((size, size), 1)
    return jnp.sum(jnp.where(here, row.astype(f32), 0.0), axis=1, keepdims=True).astype(i32)


def softplus(x):
    return jnp.maximum(x, 0.0) + jnp.log1p(jnp.exp(-jnp.abs(x)))


def fetch_kernel(
    slot_count, table_size, group_size,
    owner_hbm, row_hbm, neg_hbm, ids_hbm, type_hbm, table_hbm, center_hbm, offset_hbm,
    asked_ref, slot_ref, back_ref, block_ref, shift_ref, size_ref,
    owner_ref, row_ref, neg_ref, ids_ref, type_ref, table, center_tab, offset_tab, center_sum, offset_rows, wanted, passed, ordered, served, column,
    load_sems, first_send, first_recv, second_send, second_recv, row_send, row_recv,
    pool_send, pool_recv,
):
    hops, queries = ids_ref.shape
    width, rels = center_tab.shape
    entities = table.shape[1]
    devices = table_size * group_size
    mates = 2 * group_size
    teams = devices // mates
    row_me, col_me = lax.axis_index("table"), lax.axis_index("blk")
    me = row_me * group_size + col_me
    mate, team = lax.rem(me, mates), lax.div(me, mates)

    def target(index):
        return (lax.div(index, group_size), lax.rem(index, group_size))

    loads = [
        pltpu.make_async_copy(source, place, load_sems.at[i])
        for i, (source, place) in enumerate(
            [
                (table_hbm, table), (center_hbm, center_tab), (offset_hbm, offset_tab),
                (owner_hbm, owner_ref), (row_hbm, row_ref), (neg_hbm, neg_ref),
                (ids_hbm, ids_ref), (type_hbm, type_ref),
            ]
        )
    ]
    for load in loads[3:] + loads[:3]:
        load.start()

    barrier = pltpu.get_barrier_semaphore()

    def greet(i, _):
        pl.semaphore_signal(
            barrier, inc=1, device_id=target(lax.rem(me + i, devices)), device_id_type=MESH
        )
        return 0

    lax.fori_loop(1, devices, greet, 0)

    for load in loads[3:]:
        load.wait()
    slot, asked = plan_slots(owner_ref, row_ref, slot_count, devices, mates)
    slot_ref[...] = slot
    wanted[...] = asked.reshape(mates, teams, lanes)
    center_sum[...] = jnp.zeros_like(center_sum)
    offset_rows[...] = jnp.zeros_like(offset_rows)

    pl.semaphore_wait(barrier, devices - 1)

    def first_hop(i, _):
        other = lax.rem(mate + i, mates)
        pltpu.make_async_remote_copy(
            src_ref=wanted.at[other], dst_ref=passed.at[mate],
            send_sem=first_send, recv_sem=first_recv,
            device_id=target(team * mates + other), device_id_type=MESH,
        ).start()
        return 0

    lax.fori_loop(1, mates, first_hop, 0)

    loads[0].wait()

    def rows_at(rows):
        total = None
        for start in range(0, entities, 1024):
            hot = one_hot(iota((rows.shape[0], 1024), 1) + start == rows)
            part = dot(hot, table[:, start : start + 1024], 1, 1)
            total = part if total is None else total + part
        return total.astype(bf16)

    block_ref[0] = rows_at(column_of(neg_ref[...]))
    pool_copies = []
    for step in range(1, group_size):
        copy = pltpu.make_async_remote_copy(
            src_ref=block_ref.at[0], dst_ref=block_ref.at[step],
            send_sem=pool_send.at[step], recv_sem=pool_recv.at[step],
            device_id=(row_me, lax.rem(col_me + step, group_size)), device_id_type=MESH,
        )
        copy.start()
        pool_copies.append(copy)

    def await_all(ref, count, sem):
        part = ref.at[pl.ds(0, count)]
        pltpu.make_async_copy(part, part, sem).wait()

    def relations(base, size):
        columns = pl.ds(base, size)
        count = jnp.zeros((size, queries), f32)
        hots = []
        for hop in range(hops):
            hot = jnp.where(iota((size, queries), 0) + base == ids_ref[hop : hop + 1, :], 1.0, 0.0)
            hots.append(hot.astype(bf16))
            count = count + jnp.where(type_ref[...] >= hop, hot, 0.0)
        center_sum[...] += dot(center_tab[:, columns], count.astype(bf16), 1, 0)
        for hop in range(hops):
            here = pl.ds(hop * queries, queries)
            offset_rows[:, here] += dot(offset_tab[:, columns], hots[hop], 1, 0)

    step = 1024
    whole_steps = rels // step
    cuts = (0, 2, 4, whole_steps)

    def relations_part(i):
        def body(k, _):
            relations(pl.multiple_of(k * step, step), step)
            return 0

        lax.fori_loop(cuts[i], cuts[i + 1], body, 0)

    passed[mate] = wanted[mate]
    await_all(wanted, mates - 1, first_send)
    await_all(passed, mates - 1, first_recv)
    source, target_row = iota((devices, devices), 1), iota((devices, devices), 0)
    mate_bits, team_bits = int(math.log2(mates)), int(math.log2(teams))
    order = one_hot(
        (target_row & (mates - 1)) * teams + lax.shift_right_logical(target_row, mate_bits) == source
    )
    ordered[...] = dot(order, passed[...].reshape(devices, lanes).astype(bf16), 1, 0).reshape(
        teams, mates, lanes
    )

    def second_hop(i, _):
        other = lax.rem(team + i, teams)
        pltpu.make_async_remote_copy(
            src_ref=ordered.at[other], dst_ref=asked_ref.at[team],
            send_sem=second_send, recv_sem=second_recv,
            device_id=target(other * mates + mate), device_id_type=MESH,
        ).start()
        return 0

    lax.fori_loop(1, teams, second_hop, 0)
    loads[1].wait()
    loads[2].wait()
    relations_part(0)
    asked_ref[team] = ordered[team]
    await_all(ordered, teams - 1, second_send)
    await_all(asked_ref, teams - 1, second_recv)

    column[...] = asked_column(
        asked_ref[...].reshape(devices, lanes), slot_count,
        lambda group: partner_index(group, row_me, col_me, group_size),
    )
    quarter = devices // 4

    def send_rows(i):
        pltpu.make_async_remote_copy(
            src_ref=served.at[i], dst_ref=back_ref.at[me],
            send_sem=row_send, recv_sem=row_recv,
            device_id=partner(i, row_me, col_me), device_id_type=MESH,
        ).start()

    for part in (1, 2, 3, 0):
        size = quarter * slot_count
        rows = rows_at(column[part * size : (part + 1) * size, :])
        served[part * quarter : (part + 1) * quarter] = rows.reshape(quarter, slot_count, width)
        for i in range(max(1, part * quarter), (part + 1) * quarter):
            send_rows(i)

    back_ref[me] = served[0]
    relations_part(1)
    relations_part(2)
    if rels % step:
        relations(whole_steps * step, rels % step)
    shift_ref[...] = center_sum[...]
    total = jnp.zeros((width, queries), f32)
    for hop in range(hops):
        value = softplus(offset_rows[:, hop * queries : (hop + 1) * queries])
        total = total + jnp.where(type_ref[...] >= hop, value, 0.0)
    size_ref[...] = total
    for copy in pool_copies:
        copy.wait()
    await_all(served, devices - 1, row_send)
    await_all(back_ref, devices - 1, row_recv)


def slope_terms(gap, size):
    square = gap * gap + scaled_eps
    inverse = lax.rsqrt(square)
    spread = square * inverse
    above = 1.0 + jnp.exp2(spread - size)
    slope = (1.0 / slope_weight - pl.reciprocal(above, approx=True)) * (gap * inverse)
    return spread, above, slope


def grads_kernel(table_size, group_size, slot_ref, back_ref, block_ref, shift_ref, size_ref,
                 returned_ref, pool_ref, entity, picks, spread_out, center, size, grads, slopes, dists, weights, pool_grad, codes,
                 coded, pool_rows, row_send, row_recv, pool_send, pool_recv):
    width, queries = shift_ref.shape
    rows = back_ref.shape[0] * back_ref.shape[1]
    negatives = block_ref.shape[0] * block_ref.shape[1]
    tiles = width // 8
    devices = table_size * group_size
    row_me, col_me = lax.axis_index("table"), lax.axis_index("blk")
    me = row_me * group_size + col_me

    def target(index):
        return (lax.div(index, group_size), lax.rem(index, group_size))

    hot = one_hot(iota((rows, 2 * queries), 0) == slot_ref[...])
    picked = dot(back_ref[...].reshape(rows, width), hot, 0, 0)
    center[...] = (picked[:, 0:queries] + shift_ref[...]) * log2e
    size[...] = size_ref[...] * log2e
    grads[:, queries:] = picked[:, queries:] * log2e
    eye = one_hot(iota((negatives, negatives), 0) == iota((negatives, negatives), 1))
    columns = dot(block_ref[...].reshape(negatives, width), eye, 0, 0) * log2e
    high = columns.astype(bf16)
    entity[:, 0:negatives] = high
    entity[:, negatives:] = (columns - high.astype(f32)).astype(bf16)
    pool_grad[...] = jnp.zeros_like(pool_grad)

    spread, above, slope = slope_terms(grads[:, queries:] - center[...], size[...])
    total = jnp.sum(spread + log_weight * jnp.log2(above), axis=0, keepdims=True) * dist_unit
    weight = (loss_scale * dist_scale * slope_weight) / (1.0 + jnp.exp(margin_gamma - total))
    slope = slope * weight
    grads[:, 0:queries] = -slope
    grads[:, queries:] = slope

    halves = [pl.ds(half * lanes, lanes) for half in range(queries // lanes)]
    lane = iota((8, lanes), 1)
    group = 4
    reach = 50

    def pick(j):
        source = iota((2 * negatives, near * lanes), 0) & (negatives - 1)
        target = lax.shift_right_logical(iota(source.shape, 1), 7)
        return one_hot(source == j * near + target)

    spread_out[0] = dot(entity[...], pick(0), 1, 0)

    def chunk(j, _):
        here = j * near
        now = lax.rem(j, 2)
        for first in range(0, near, group):
            def forward(base, count, sums):
                sums = list(sums)
                for k in range(group):
                    at = first + k
                    for half, ql in enumerate(halves):
                        total = sums[half * group + k]
                        product = None
                        for tile in range(count):
                            d = pl.ds(base + tile * 8, 8)
                            column = spread_out[now, d, at * lanes : (at + 1) * lanes]
                            spread, above, slope = slope_terms(column - center[d, ql], size[d, ql])
                            slopes[at, d, ql] = slope
                            product = above if product is None else product * above
                            total = total + spread
                            if tile % 4 == 3 or tile == count - 1:
                                total = total + log_weight * jnp.log2(product)
                                product = None
                        sums[half * group + k] = total
                return tuple(sums)

            sums = tuple(jnp.zeros((8, lanes), f32) for _ in range(group * len(halves)))
            for start in range(0, tiles, reach):
                sums = forward(start * 8, min(reach, tiles - start), sums)
            for half, ql in enumerate(halves):
                for k in range(group):
                    dists[first + k : first + k + 1, ql] = jnp.sum(
                        sums[half * group + k], axis=0, keepdims=True
                    )
        scale = -loss_scale * dist_scale * slope_weight / negatives
        weights[...] = scale / (1.0 + jnp.exp(dists[...] * dist_unit - margin_gamma))
        weight_rows = [
            [jnp.broadcast_to(weights[k : k + 1, ql], (8, lanes)) for ql in halves]
            for k in range(near)
        ]

        picks[...] = pick(j + 1)

        spread_out[1 - now] = dot(entity[...], picks[...], 1, 0)
        for tile in range(tiles):
            d = pl.ds(tile * 8, 8)
            to_center = [grads[d, ql] for ql in halves]
            to_pool = pool_grad[d, :]
            for k in range(near):
                row = None
                for half, ql in enumerate(halves):
                    term = slopes[k, d, ql] * weight_rows[k][half]
                    to_center[half] = to_center[half] - term
                    row = term if row is None else row + term
                row = jnp.sum(row, axis=1, keepdims=True)
                to_pool = jnp.where(lane == here + k, row, to_pool)
            for half, ql in enumerate(halves):
                grads[d, ql] = to_center[half]
            pool_grad[d, :] = to_pool
        return 0

    lax.fori_loop(0, negatives // near, chunk, 0)

    value = grads[...]
    most = jnp.max(jnp.abs(value), axis=0, keepdims=True)
    power = 14.0 - jnp.floor(jnp.log2(jnp.maximum(most, 1e-30)))
    level = jnp.minimum(jnp.maximum(jnp.round(value * jnp.exp2(power)), -32767.0), 32767.0)
    high = jnp.floor(level * (1.0 / 256.0) + 0.5)
    low = level - high * 256.0
    codes[...] = jnp.zeros_like(codes)
    codes[0:width, 0 : 2 * queries] = high.astype(bf16)
    codes[0:width, 2 * queries :] = low.astype(bf16)
    codes[width : width + 16, 2 * queries :] = jnp.broadcast_to(power, (16, 2 * queries)).astype(bf16)
    for step in range(group_size):
        pool_rows[step] = jnp.transpose(
            pool_grad[...]
        )[step * negatives // group_size : (step + 1) * negatives // group_size, 0:width]
    copies = []
    for step in range(1, group_size):
        copy = pltpu.make_async_remote_copy(
            src_ref=pool_rows.at[step], dst_ref=pool_ref.at[step],
            send_sem=pool_send.at[step], recv_sem=pool_recv.at[step],
            device_id=(row_me, lax.rem(col_me + group_size - step, group_size)),
            device_id_type=MESH,
        )
        copy.start()
        copies.append(copy)

    slot_count = rows // devices
    quarter = devices // 4

    def send_rows(i):
        pltpu.make_async_remote_copy(
            src_ref=coded.at[i], dst_ref=returned_ref.at[me],
            send_sem=row_send, recv_sem=row_recv,
            device_id=partner(i, row_me, col_me), device_id_type=MESH,
        ).start()

    for part in range(4):
        size = quarter * slot_count
        place = iota((size, 1), 0) + part * size
        group = lax.shift_right_logical(place, int(math.log2(slot_count)))
        place = (place & (slot_count - 1)) + slot_count * partner_index(
            group, row_me, col_me, group_size
        )
        chosen = one_hot(place == slot_ref[...])
        level = dot(chosen, codes[:, 0 : 2 * queries], 1, 1) * 256.0
        level = level + dot(chosen, codes[:, 2 * queries :], 1, 1)
        level = level.astype(i32).astype(jnp.int16)
        coded[part * quarter : (part + 1) * quarter] = level.reshape(
            quarter, slot_count, codes.shape[0]
        )
        for i in range(max(1, part * quarter), (part + 1) * quarter):
            send_rows(i)

    returned_ref[me] = coded[0]
    pool_ref[0] = pool_rows[0]
    for copy in copies:
        copy.wait()
    sent, got = coded.at[pl.ds(0, devices - 1)], returned_ref.at[pl.ds(0, devices - 1)]
    pltpu.make_async_copy(sent, sent, row_send).wait()
    pltpu.make_async_copy(got, got, row_recv).wait()


def step_kernel(slot_count, table_size, group_size, *refs):
    sources, (asked_ref, returned_ref, pool_ref), scratch = refs[0:8], refs[8:11], refs[11:]
    boxes, fetching, grading = scratch[0:5], scratch[5:29], scratch[29:]
    fetch_kernel(slot_count, table_size, group_size, *sources, asked_ref, *boxes, *fetching)
    grads_kernel(table_size, group_size, *boxes, returned_ref, pool_ref, *grading)


def step(owner, row, neg_row, rel_ids, query_type, table, rel_center, rel_offset, slot_count,
         table_size, group_size):
    hops, queries = rel_ids.shape
    width, rels = rel_center.shape
    entities = table.shape[1]
    devices = table_size * group_size
    mates = 2 * group_size
    teams = devices // mates
    pool = neg_row.shape[1]
    negatives = group_size * pool
    padded = -(-width // lanes) * lanes
    dma = pltpu.SemaphoreType.DMA
    boxes = [
        pltpu.VMEM((1, 2 * queries), i32),
        pltpu.VMEM((devices, slot_count, width), bf16),
        pltpu.VMEM((group_size, pool, width), bf16),
        pltpu.VMEM((width, queries), f32),
        pltpu.VMEM((width, queries), f32),
    ]
    fetching = [
        pltpu.VMEM(owner.shape, i32),
        pltpu.VMEM(row.shape, i32),
        pltpu.VMEM(neg_row.shape, i32),
        pltpu.VMEM(rel_ids.shape, i32),
        pltpu.VMEM(query_type.shape, i32),
        pltpu.VMEM((width, entities), bf16),
        pltpu.VMEM((width, rels), bf16),
        pltpu.VMEM((width, rels), bf16),
        pltpu.VMEM((width, queries), f32),
        pltpu.VMEM((width, hops * queries), f32),
        pltpu.VMEM((mates, teams, lanes), f32),
        pltpu.VMEM((mates, teams, lanes), f32),
        pltpu.VMEM((teams, mates, lanes), f32),
        pltpu.VMEM((devices, slot_count, width), bf16),
        pltpu.VMEM((devices * slot_count, 1), i32),
        dma((8,)), dma, dma, dma, dma, dma, dma, dma((group_size,)), dma((group_size,)),
    ]
    grading = [
        pltpu.VMEM((width, 2 * negatives), bf16),
        pltpu.VMEM((2 * negatives, near * lanes), bf16),
        pltpu.VMEM((2, width, near * lanes), f32),
        pltpu.VMEM((width, queries), f32),
        pltpu.VMEM((width, queries), f32),
        pltpu.VMEM((width, 2 * queries), f32),
        pltpu.VMEM((near, width, queries), f32),
        pltpu.VMEM((near, queries), f32),
        pltpu.VMEM((near, queries), f32),
        pltpu.VMEM((padded, negatives), f32),
        pltpu.VMEM((padded, 4 * queries), bf16),
        pltpu.VMEM((devices, slot_count, padded), jnp.int16),
        pltpu.VMEM((group_size, pool, width), f32),
        dma, dma, dma((group_size,)), dma((group_size,)),
    ]
    scratch = boxes + fetching + grading
    return pl.pallas_call(
        functools.partial(step_kernel, slot_count, table_size, group_size),
        out_shape=(
            jax.ShapeDtypeStruct((teams, mates, lanes), f32),
            jax.ShapeDtypeStruct((devices, slot_count, padded), jnp.int16),
            jax.ShapeDtypeStruct((group_size, pool, width), f32),
        ),
        in_specs=[pl.BlockSpec(memory_space=pltpu.HBM)] * 8,
        out_specs=(whole(),) * 3,
        scratch_shapes=scratch,
        compiler_params=params(56, collective_id=0, has_side_effects=True),
        name="step",
    )(owner, row, neg_row, rel_ids, query_type, table, rel_center, rel_offset)


def scatter_kernel(slot_count, asked_hbm, neg_hbm, back_hbm, pool_hbm, out_ref,
                   asked_ref, neg_ref, back_ref, pool_ref, column, rows_of, both, sems):
    step = pl.program_id(0)
    width, part = out_ref.shape
    rows, padded = back_ref.shape
    group_size, pool = pool_ref.shape[0:2]

    @pl.when(step == 0)
    def _():
        loads = [
            pltpu.make_async_copy(source, place, sems.at[i])
            for i, (source, place) in enumerate(
                [
                    (asked_hbm, asked_ref), (neg_hbm, neg_ref), (back_hbm, back_ref),
                    (pool_hbm, pool_ref),
                ]
            )
        ]
        for load in loads:
            load.start()
        loads[0].wait()
        column[0:rows, :] = asked_column(asked_ref[...], slot_count)
        loads[1].wait()
        column[rows : rows + pool, :] = column_of(neg_ref[...])
        column[rows + pool :, :] = jnp.full((lanes - pool, 1), -1, i32)
        loads[2].wait()
        level = back_ref[...].astype(i32).astype(f32)
        rows_of[0:rows, :] = level * jnp.exp2(-level[:, width : width + 1])
        rows_of[rows:, :] = jnp.zeros((lanes, padded), f32)
        loads[3].wait()
        rows_of[rows : rows + pool, 0:width] = sum(pool_ref[i] for i in range(group_size))
        value = jnp.transpose(rows_of[...])[0:width, :]
        high = value.astype(bf16)
        both[0:width, :] = high
        both[width:, :] = (value - high.astype(f32)).astype(bf16)

    hot = one_hot(iota((rows + lanes, part), 1) == column[...] - step * part)
    result = dot(both[...], hot, 1, 0)
    out_ref[...] = result[0:width, :] + result[width:, :]


def scatter(asked, neg_rows, back, pools, slot_count, entities):
    rows, padded = back.shape
    pool = neg_rows.shape[1]
    width = pools.shape[2]
    part = 1024
    return pl.pallas_call(
        functools.partial(scatter_kernel, slot_count),
        out_shape=jax.ShapeDtypeStruct((width, entities), f32),
        grid=(entities // part,),
        in_specs=[pl.BlockSpec(memory_space=pltpu.HBM)] * 4,
        out_specs=pl.BlockSpec((width, part), lambda i: (0, i)),
        scratch_shapes=[
            pltpu.VMEM(asked.shape, f32),
            pltpu.VMEM(neg_rows.shape, i32),
            pltpu.VMEM(back.shape, jnp.int16),
            pltpu.VMEM(pools.shape, f32),
            pltpu.VMEM((rows + lanes, 1), i32),
            pltpu.VMEM((rows + lanes, padded), f32),
            pltpu.VMEM((2 * width, rows + lanes), bf16),
            pltpu.SemaphoreType.DMA((4,)),
        ],
        compiler_params=params(56),
        name="scatter",
    )(asked, neg_rows, back, pools)


def local(
    entity_table, rel_center, rel_offset, entity_owner, entity_row, rel_ids, query_type, neg_rows
):
    entities, width = entity_table.shape
    table_size = lax.axis_size("table")
    group_size = lax.axis_size("blk")
    devices = table_size * group_size
    queries = rel_ids.shape[0]
    slot_count = 4 * queries // devices
    pool = neg_rows.shape[0]
    table = entity_table.T
    neg_row = neg_rows.reshape(1, pool)
    asked, returned, pool_grads = step(
        entity_owner.transpose(1, 2, 0), entity_row.T, neg_row, rel_ids.T,
        query_type.reshape(1, queries), table, rel_center.T, rel_offset.T, slot_count,
        table_size, group_size,
    )
    asked = asked.reshape(devices, lanes)
    returned = returned.reshape(devices * slot_count, -1)
    return scatter(asked, neg_row, returned, pool_grads, slot_count, entities).T


def solution(mesh):
    placed = (
        P(("table", "blk"), None),
        P(),
        P(),
        P(("table", "blk"), None, None),
        P(("table", "blk"), None),
        P(("table", "blk"), None),
        P(("table", "blk")),
        P(("table", "blk")),
    )
    return jax.shard_map(
        local, mesh=mesh, in_specs=placed, out_specs=P(("table", "blk"), None), check_vma=False
    )
```
